32 devices in a mesh: row: 8 (over z, y), col: 4 (over x, core).
Axes of the slice: x: 2, y: 2, z: 4, core: 2. Of those that a mesh axis runs over, the one named last changes fastest.
Arguments:
- features: bfloat16 [4, 4096, 128], P('col', 'row'), may hold values from -6 to 6
- weight1: bfloat16 [128, 128], replicated, may hold values from -0.5 to 0.5
- weight2: bfloat16 [128, 128], replicated, may hold values from -0.5 to 0.5
- tile_values: bfloat16 [8, 4, 96, 128, 128], P('row', 'col'), may hold values from -0.375 to 0.375
- tile_coords: int32 [8, 4, 2, 96], P('row', 'col'), may hold values from 0 to 31, as said below
- tile_count: int32 [8, 4], P('row', 'col'), may hold values from 1 to 96, as said below
- out_grad: bfloat16 [4, 4096, 128], P('col', 'row'), may hold values from -6 to 6
Outputs:
- output: bfloat16 [4, 4096, 128], P('col', 'row')
- grad_features: bfloat16 [4, 4096, 128], P('col', 'row')
- grad_weight1: float32 [128, 128], replicated
- grad_weight2: float32 [128, 128], replicated
The draws below stay inside these ranges and needn't reach their ends.
Inputs may be any that keep to these rules, and one draw needn't show every extreme that they name: On each device tile_coords[r, c, 0, t] is below 16 and tile_coords[r, c, 1, t] below 32; no block position appears twice among a device's 96 slots. `tile_count`: some device has all 96 slots live.
All inputs are finite; a program needn't handle non-finite values.
Results may differ from the reference program's by a relative error of at most 0.034.
Values may be sent and summed in bfloat16 or wider, within the bound.
A program may use at most 64 MiB of HBM per device.

```python
import jax
import jax.numpy as jnp
from jax import lax

F = 128
BLK = 128
RB = 16
TILES_DEV = 96
ROW_SHARDS = 8
COL_SHARDS = 4
CB = 32
NODES = 16384


def draw_tile_coords(key, part):
    device_keys = jax.random.split(key, ROW_SHARDS * COL_SHARDS)

    def one_device(sub_key):
        places = jax.random.permutation(sub_key, RB * CB)[:TILES_DEV]
        return jnp.stack([places // CB, places % CB])
    coords = jax.vmap(one_device)(device_keys)
    return coords.reshape(ROW_SHARDS, COL_SHARDS, 2, TILES_DEV).astype(jnp.int32)


def draw_tile_count(key, part):
    key_shift, key_jitter, key_full = jax.random.split(key, 3)
    grid_shape = (ROW_SHARDS, COL_SHARDS)
    shifts = jax.random.randint(key_shift, grid_shape, 0, 3)
    base_count = jnp.right_shift(jnp.full(grid_shape, TILES_DEV, jnp.int32), shifts.astype(jnp.int32))
    jitter = jax.random.randint(key_jitter, grid_shape, 0, 65536).astype(jnp.int32) % (base_count // 4 + 1)
    counts = base_count - jitter
    chosen = jax.random.randint(key_full, (), 0, ROW_SHARDS * COL_SHARDS).astype(jnp.int32)
    flat_ids = jnp.arange(ROW_SHARDS * COL_SHARDS, dtype=jnp.int32).reshape(grid_shape)
    return jnp.where(flat_ids == chosen, TILES_DEV, counts).astype(jnp.int32)


def block_levels(key, shape, cuts, least, top_value):
    def one(axis_at, parts):
        draws = jax.random.uniform(jax.random.fold_in(jax.random.fold_in(key, 6), axis_at), (parts,), jnp.float32, least / len(cuts), top_value / len(cuts))
        return jnp.repeat(jnp.exp(draws), shape[axis_at] // parts).reshape((-1,) + (1,) * (len(shape) - axis_at - 1))

    loudness = one(*cuts[0])
    for cut in cuts[1:]:
        loudness = loudness * one(*cut)
    return loudness


def gaussian(key, dims, deviation, most, shards=(), held_as=jnp.bfloat16):
    level = block_levels(key, dims, shards, -0.22, 0.18) if shards else 1.0
    entries = jax.random.normal(key, dims, jnp.float32) * deviation * level
    return jnp.minimum(jnp.maximum(entries, -most), most).astype(held_as)


def setup_inputs(seed: int = 0) -> dict:
    arg_keys = jax.random.split(jax.random.key(seed), 8)
    return {
        "features": gaussian(arg_keys[0], (COL_SHARDS, CB * BLK, F), 1.0, 6.0, ((0, 4), (1, 8))),
        "weight1": gaussian(arg_keys[1], (F, F), F ** -0.5, 0.5),
        "weight2": gaussian(arg_keys[2], (F, F), F ** -0.5, 0.5),
        "tile_values": gaussian(arg_keys[3], (ROW_SHARDS, COL_SHARDS, TILES_DEV, BLK, BLK), (1.4 / (BLK * TILES_DEV * COL_SHARDS // RB) ** 0.5), 0.375, ((0, 8), (1, 4))),
        "tile_coords": draw_tile_coords(jax.random.fold_in(arg_keys[7], 71), 0),
        "tile_count": draw_tile_count(jax.random.fold_in(arg_keys[7], 71), 0),
        "out_grad": gaussian(arg_keys[6], (COL_SHARDS, CB * BLK, F), 1.0, 6.0, ((0, 4), (1, 8))),
    }


def forward_part(tile_block, coord_block, live_count, panel_rows):
    blocks = panel_rows.reshape(CB, BLK, F)[coord_block[1]]
    products = jnp.einsum("tij,tjf->tif", tile_block.astype(jnp.float32), blocks.astype(jnp.float32))
    live_slots = jnp.arange(TILES_DEV) < live_count
    onehot = jnp.where((coord_block[0][None, :] == jnp.arange(RB)[:, None]) & live_slots[None, :], 1.0, 0.0).astype(jnp.float32)
    return jnp.einsum("rt,tif->rif", onehot, products).reshape(RB * BLK, F)


def transposed_part(tile_block, coord_block, live_count, panel_rows):
    blocks = panel_rows.reshape(RB, BLK, F)[coord_block[0]]
    products = jnp.einsum("tji,tjf->tif", tile_block.astype(jnp.float32), blocks.astype(jnp.float32))
    live_slots = jnp.arange(TILES_DEV) < live_count
    onehot = jnp.where((coord_block[1][None, :] == jnp.arange(CB)[:, None]) & live_slots[None, :], 1.0, 0.0).astype(jnp.float32)
    return jnp.einsum("ct,tif->cif", onehot, products).reshape(CB * BLK, F)


def rounded(value):
    return lax.optimization_barrier(value.astype(jnp.bfloat16)).astype(jnp.float32)


def rows_sum(tile_values, tile_coords, tile_count, col_panels):
    def per_row(row_id):
        def per_col(col_id):
            return rounded(forward_part(tile_values[row_id, col_id], tile_coords[row_id, col_id], tile_count[row_id, col_id], col_panels[col_id]))
        return jnp.sum(lax.map(per_col, jnp.arange(COL_SHARDS)), axis=0)
    return lax.map(per_row, jnp.arange(ROW_SHARDS))


def cols_sum(tile_values, tile_coords, tile_count, row_panels):
    def per_col(col_id):
        def per_row(row_id):
            return rounded(transposed_part(tile_values[row_id, col_id], tile_coords[row_id, col_id], tile_count[row_id, col_id], row_panels[row_id]))
        return jnp.sum(lax.map(per_row, jnp.arange(ROW_SHARDS)), axis=0)
    return lax.map(per_col, jnp.arange(COL_SHARDS))


def silu_slope(value):
    sigmoid = jax.nn.sigmoid(value)
    return sigmoid * (1.0 + value * (1.0 - sigmoid))


def reference(features, weight1, weight2, tile_values, tile_coords, tile_count, out_grad):
    agg_one = rows_sum(tile_values, tile_coords, tile_count, features).astype(jnp.bfloat16).reshape(NODES, F)
    pre_one = jnp.dot(agg_one, weight1, preferred_element_type=jnp.float32)
    hidden = jax.nn.silu(pre_one).astype(jnp.bfloat16)
    agg_two = cols_sum(tile_values, tile_coords, tile_count, hidden.reshape(ROW_SHARDS, RB * BLK, F)).astype(jnp.bfloat16).reshape(NODES, F)
    output = jnp.dot(agg_two, weight2, preferred_element_type=jnp.float32).astype(jnp.bfloat16)
    grad_flat = out_grad.reshape(NODES, F)
    grad_two = jnp.dot(grad_flat, weight2.T, preferred_element_type=jnp.float32).astype(jnp.bfloat16)
    grad_hidden = rows_sum(tile_values, tile_coords, tile_count, grad_two.reshape(COL_SHARDS, CB * BLK, F)).reshape(NODES, F)
    grad_pre = (grad_hidden * silu_slope(pre_one)).astype(jnp.bfloat16)
    grad_one = jnp.dot(grad_pre, weight1.T, preferred_element_type=jnp.float32).astype(jnp.bfloat16)
    grad_features = cols_sum(tile_values, tile_coords, tile_count, grad_one.reshape(ROW_SHARDS, RB * BLK, F)).astype(jnp.bfloat16)
    factor = 1.0 / (NODES ** 0.5)
    grad_weight1 = jnp.dot(agg_one.T, grad_pre, preferred_element_type=jnp.float32) * factor
    grad_weight2 = jnp.dot(agg_two.T, grad_flat, preferred_element_type=jnp.float32) * factor
    return (output.reshape(COL_SHARDS, CB * BLK, F), grad_features, grad_weight1, grad_weight2)
```

```python
import functools
import math

import jax
import jax.numpy as jnp
from jax import lax
from jax.experimental import pallas as pl
from jax.experimental.pallas import tpu as pltpu
from jax.sharding import PartitionSpec as P

MESH = pl.DeviceIdType.MESH
BF16 = jnp.bfloat16
F32 = jnp.float32


def dot(a, b, dims=((1,), (0,))):
    return lax.dot_general(a, b, (dims, ((), ())), preferred_element_type=F32)


def kernel(
    nr, nc, factor,
    slot_ref, feat_ref, grad_ref, w1_ref, w2_ref, tiles_hbm,
    out_ref, gf_ref, gw1_ref, gw2_ref,
    tiles, dense, xs, part, psend, precv, pre, hid, agg, zt,
    ybuf, yrecv, zbuf, zrecv, gsend, grecv, gsum, gfin,
    tile_sem, xss, xrs, pss, prs, tss, trs, yss, yrs, zss, zrs,
    g1s, g1r, g2s, g2r, g3s, g3r,
):
    shard, width = feat_ref.shape
    blk = tiles.shape[1]
    panel = dense.shape[1]
    n_tiles = tiles.shape[0] - 1
    zn = nr // 2
    r, c = lax.axis_index("row"), lax.axis_index("col")
    z, y = r // 2, r % 2
    mate = z * 2 + (1 - y)
    piece = 2 * width // nc

    tile_copy = pltpu.make_async_copy(tiles_hbm, tiles.at[pl.ds(0, n_tiles)], tile_sem)
    tile_copy.start()
    xs[0, r] = feat_ref[...]
    xs[1, r] = grad_ref[...]

    barrier = pltpu.get_barrier_semaphore()

    def greet(axis, n, me):
        def body(k, _):
            pl.semaphore_signal(barrier, inc=1, device_id={axis: (me + k) % n}, device_id_type=MESH)
            return 0
        lax.fori_loop(1, n, body, 0)
    greet("row", nr, r)
    greet("col", nc, c)
    pl.semaphore_wait(barrier, nr - 1 + nc - 1)

    def remote(src, dst, ss, rs, axis, target):
        return pltpu.make_async_remote_copy(
            src_ref=src, dst_ref=dst, send_sem=ss, recv_sem=rs,
            device_id={axis: target}, device_id_type=MESH)

    def x_copy(h, idx, way):
        target = (r + 2, r - 2, mate)[way]
        return remote(xs.at[h, idx], xs.at[h, idx], xss.at[h, idx, way], xrs.at[h, idx], "row", target)

    def x_forward(h, idx, sign, act):
        @pl.when(sign > 0)
        def _():
            @pl.when(z < zn - 1)
            def _():
                act(x_copy(h, idx, 0))

        @pl.when(sign < 0)
        def _():
            @pl.when(z > 0)
            def _():
                act(x_copy(h, idx, 1))

    def start(copy):
        copy.start()

    def wait_send(copy):
        copy.wait_send()

    def x_own(h, act):
        act(x_copy(h, r, 2))

        @pl.when(z < zn - 1)
        def _():
            act(x_copy(h, r, 0))

        @pl.when(z > 0)
        def _():
            act(x_copy(h, r, 1))

    rows_step = 512

    def accumulate(h, idx, first=False):
        def body(m, _):
            rows = pl.ds(pl.multiple_of(m * rows_step, rows_step), rows_step)
            add = dot(dense[idx, rows, :], xs[h, idx])
            part[h, rows, :] = add if first else part[h, rows, :] + add
            return 0
        lax.fori_loop(0, panel // rows_step, body, 0)

    def x_pass(h, s):
        def body(q, _):
            sign = 1 - 2 * q
            zz = z - sign * s

            @pl.when((zz >= 0) & (zz < zn))
            def _():
                idx = zz * 2 + y
                x_copy(h, idx, 2).wait_recv()
                x_forward(h, idx, sign, start)
                x_copy(h, idx, 2).start()
            return 0
        lax.fori_loop(0, 2, body, 0)

    def x_use(h, s):
        def body(q, _):
            late = q // 2
            sign = 2 * (q % 2) - 1
            zz = z + sign * (s - late)
            yy = y + late * (1 - 2 * y)

            @pl.when((zz >= 0) & (zz < zn) & ((q < 3) | (s > 1)))
            def _():
                idx = zz * 2 + yy

                @pl.when(late == 1)
                def _():
                    x_copy(h, idx, 2).wait_recv()
                accumulate(h, idx)
            return 0
        lax.fori_loop(0, 4, body, 0)

    def x_steps(h, lo, hi):
        def body(s, _):
            x_pass(h, s)
            x_use(h, s)
            return 0
        lax.fori_loop(lo, hi, body, 0)

    def x_drain(h):
        x_own(h, wait_send)

        def body(k, _):
            q, s = k % 2, k // 2 + 1
            sign = 1 - 2 * q
            zz = z - sign * s

            @pl.when((zz >= 0) & (zz < zn))
            def _():
                idx = zz * 2 + y
                x_forward(h, idx, sign, wait_send)
                x_copy(h, idx, 2).wait_send()
            return 0
        lax.fori_loop(0, 2 * (zn - 1), body, 0)

    def peers(n, me, act):
        def body(k, _):
            act((me + k) % n)
            return 0
        lax.fori_loop(1, n, body, 0)

    def p_copy(h, peer, src):
        return remote(psend.at[h, peer], precv.at[h, src], pss.at[h, peer], prs.at[h, src], "col", peer)

    def own_rows():
        return pl.ds(pl.multiple_of(c * shard, shard), shard)

    def p_send(h):
        def act(peer):
            rows = pl.ds(pl.multiple_of(peer * shard, shard), shard)
            psend[h, peer] = part[h, rows, :].astype(BF16)
            p_copy(h, peer, c).start()
        peers(nc, c, act)

    def p_sum(h):
        agg[h] = part[h, own_rows(), :].astype(BF16).astype(F32)

        def act(peer):
            p_copy(h, peer, peer).wait_recv()
            agg[h] = agg[h] + precv[h, peer].astype(F32)
        peers(nc, c, act)
        return agg[h]

    def t_copy(h, peer, src):
        return remote(zt.at[h, src], zt.at[h, src], tss.at[h, peer], trs.at[h, src], "col", peer)

    def z_send(h, value):
        zt[h, c] = value.T.astype(BF16)
        peers(nc, c, lambda peer: t_copy(h, peer, c).start())

    def z_wait(h):
        peers(nc, c, lambda peer: t_copy(h, peer, peer).wait_recv())

    def product(h, idx):
        total = dot(zt[h, 0], dense[idx, 0:shard, :])
        for k in range(1, nc):
            total = total + dot(zt[h, k], dense[idx, k * shard:(k + 1) * shard, :])
        return total

    def y_copy(h, zd):
        return remote(ybuf.at[h, zd], yrecv.at[h, zd], yss.at[h, zd], yrs.at[h, zd], "row", mate)

    def z_copy(h, zd, side):
        target = (r + 2, r - 2)[side]
        return remote(zbuf.at[h, zd], zrecv.at[h, side, zd], zss.at[h, zd], zrs.at[h, side, zd], "row", target)

    def both(d, act):
        def body(q, _):
            zd = z + (2 * q - 1) * d

            @pl.when((zd >= 0) & (zd < zn) & ((q == 0) | (d > 0)))
            def _():
                act(zd)
            return 0
        lax.fori_loop(0, 2, body, 0)

    def y_part(h, d):
        def act(zd):
            ybuf[h, zd] = product(h, zd * 2 + (1 - y)).astype(BF16)
            y_copy(h, zd).start()
        both(d, act)

    def z_part(h, d, total):
        def act(zd):
            total[...] = product(h, zd * 2 + y)
            y_copy(h, zd).wait_recv()
            total[...] = total[...] + yrecv[h, zd].astype(F32)

            @pl.when((z > 0) & (zd >= z))
            def _():
                z_copy(h, zd, 0).wait_recv()
                total[...] = total[...] + zrecv[h, 0, zd].astype(F32)

            @pl.when((z < zn - 1) & (zd <= z))
            def _():
                z_copy(h, zd, 1).wait_recv()
                total[...] = total[...] + zrecv[h, 1, zd].astype(F32)

            @pl.when(zd != z)
            def _():
                zbuf[h, zd] = total[...].astype(BF16)

            @pl.when(zd > z)
            def _():
                z_copy(h, zd, 0).start()

            @pl.when(zd < z)
            def _():
                z_copy(h, zd, 1).start()
        both(d, act)

    def b_steps(h, lo, hi, total):
        def body(i, _):
            @pl.when(i < zn)
            def _():
                y_part(h, zn - 1 - i)

            @pl.when(i >= 1)
            def _():
                z_part(h, zn - i, total)
            return 0
        lax.fori_loop(lo, hi, body, 0)

    def b_drain(h):
        def body(zd, _):
            y_copy(h, zd).wait_send()

            @pl.when(zd > z)
            def _():
                z_copy(h, zd, 0).wait_send()

            @pl.when(zd < z)
            def _():
                z_copy(h, zd, 1).wait_send()
            return 0
        lax.fori_loop(0, zn, body, 0)

    def g1_copy(peer, src):
        return remote(gsend.at[peer], grecv.at[src], g1s.at[peer], g1r.at[src], "col", peer)

    def g2_copy(peer, src):
        return remote(gsum.at[src], gsum.at[src], g2s.at[peer], g2r.at[src], "row", peer)

    def g3_copy(peer, src):
        return remote(gfin.at[src], gfin.at[src], g3s.at[peer], g3r.at[src], "col", peer)

    x_own(0, start)
    tiles[n_tiles] = jnp.zeros((blk, blk), BF16)
    tile_copy.wait()
    per = shard // blk
    n_rows = panel // blk

    def fill(i, _):
        k, row = i // n_rows, i % n_rows
        rows = pl.ds(pl.multiple_of(row * blk, blk), blk)
        for b in range(per):
            slot = slot_ref[row * (nr * per) + k * per + b]
            dense[k, rows, b * blk:(b + 1) * blk] = tiles[slot]
        return 0
    lax.fori_loop(0, nr * n_rows, fill, 0)

    accumulate(0, r, True)
    x_steps(0, 1, zn)
    x_own(1, start)
    x_use(0, zn)
    p_send(0)
    accumulate(1, r, True)
    x_steps(1, 1, 2)

    agg_one = p_sum(0).astype(BF16)
    pre_one = dot(agg_one, w1_ref[...])
    pre[...] = pre_one
    hidden = (pre_one / (1.0 + jnp.exp(-pre_one))).astype(BF16)
    hid[...] = hidden
    z_send(0, dot(hidden, w2_ref[...]))

    x_steps(1, 2, zn)
    x_use(1, zn)
    p_send(1)
    z_wait(0)

    def with_total(total):
        b_steps(0, 0, 2, total)

        agg_grad = p_sum(1).astype(BF16)
        pre_one = pre[...]
        s = 1.0 / (1.0 + jnp.exp(-pre_one))
        slope = s * (1.0 + pre_one * (1.0 - s))
        grad_pre = (dot(agg_grad, w2_ref[...], ((1,), (1,))) * slope).astype(BF16)
        z_send(1, dot(grad_pre, w1_ref[...], ((1,), (1,))))
        one = dot(agg[0].T.astype(BF16), grad_pre) * factor
        two = dot(hid[...].astype(F32).T.astype(BF16), agg_grad) * factor
        for k in range(nc):
            lo = k * piece
            half = one if lo < width else two
            gsend[k] = half[lo % width:lo % width + piece].astype(BF16)
        peers(nc, c, lambda peer: g1_copy(peer, c).start())

        b_steps(0, 2, zn + 1, total)
        out_ref[...] = total[...].T.astype(BF16)

        mine = gsend[c].astype(F32)
        gfin[c] = mine

        def add_piece(peer):
            g1_copy(peer, peer).wait_recv()
            gfin[c] = gfin[c] + grecv[peer].astype(F32)
        peers(nc, c, add_piece)
        gsum[r] = gfin[c].astype(BF16)
        peers(nr, r, lambda peer: g2_copy(peer, r).start())

        z_wait(1)
        b_steps(1, 0, 2, total)

        peers(nr, r, lambda peer: g2_copy(peer, peer).wait_recv())
        gfin[c] = gsum[0].astype(F32)

        def add_row(k, _):
            gfin[c] = gfin[c] + gsum[k].astype(F32)
            return 0
        lax.fori_loop(1, nr, add_row, 0)
        peers(nc, c, lambda peer: g3_copy(peer, c).start())

        b_steps(1, 2, zn + 1, total)
        gf_ref[...] = total[...].T.astype(BF16)

    pl.run_scoped(with_total, pltpu.VMEM((width, shard), F32))

    peers(nc, c, lambda peer: g3_copy(peer, peer).wait_recv())
    for k in range(nc):
        lo = k * piece
        ref = gw1_ref if lo < width else gw2_ref
        ref[lo % width:lo % width + piece, :] = gfin[k]

    for h in range(2):
        x_drain(h)
        peers(nc, c, lambda peer: p_copy(h, peer, c).wait_send())
        peers(nc, c, lambda peer: t_copy(h, peer, c).wait_send())
        b_drain(h)
    peers(nc, c, lambda peer: g1_copy(peer, c).wait_send())
    peers(nr, r, lambda peer: g2_copy(peer, r).wait_send())
    peers(nc, c, lambda peer: g3_copy(peer, c).wait_send())


def on_device(nr, nc, features, weight1, weight2, tile_values, tile_coords, tile_count, out_grad):
    local_tiles = tile_values[0, 0]
    n_tiles, blk = local_tiles.shape[:2]
    shard, width = features.shape[1:]
    panel, col_blocks = shard * nc, shard * nr // blk
    row_blocks = panel // blk
    slots = jnp.arange(n_tiles, dtype=jnp.int32)
    place = tile_coords[0, 0, 0] * col_blocks + tile_coords[0, 0, 1]
    live = slots < tile_count[0, 0]
    hit = (place[None, :] == jnp.arange(row_blocks * col_blocks, dtype=jnp.int32)[:, None]) & live[None, :]
    slot_map = n_tiles + jnp.sum(jnp.where(hit, slots[None, :] - n_tiles, 0), axis=1)
    zn = nr // 2
    piece = 2 * width // nc
    factor = 1.0 / math.sqrt(shard * nr * nc)
    vmem, dma = pltpu.VMEM, pltpu.SemaphoreType.DMA
    in_vmem = pl.BlockSpec(memory_space=pltpu.VMEM)
    output, grad_features, gw1, gw2 = pl.pallas_call(
        functools.partial(kernel, nr, nc, factor),
        out_shape=(
            jax.ShapeDtypeStruct((shard, width), BF16),
            jax.ShapeDtypeStruct((shard, width), BF16),
            jax.ShapeDtypeStruct((width, width), F32),
            jax.ShapeDtypeStruct((width, width), F32),
        ),
        in_specs=[pl.BlockSpec(memory_space=pltpu.SMEM)] + [in_vmem] * 4 + [pl.BlockSpec(memory_space=pl.ANY)],
        out_specs=(in_vmem,) * 4,
        scratch_shapes=[
            vmem((n_tiles + 1, blk, blk), BF16),
            vmem((nr, panel, shard), BF16),
            vmem((2, nr, shard, width), BF16),
            vmem((2, panel, width), F32),
            vmem((2, nc, shard, width), BF16),
            vmem((2, nc, shard, width), BF16),
            vmem((shard, width), F32),
            vmem((shard, width), BF16),
            vmem((2, shard, width), F32),
            vmem((2, nc, width, shard), BF16),
            vmem((2, zn, width, shard), BF16),
            vmem((2, zn, width, shard), BF16),
            vmem((2, zn, width, shard), BF16),
            vmem((2, 2, zn, width, shard), BF16),
            vmem((nc, piece, width), BF16),
            vmem((nc, piece, width), BF16),
            vmem((nr, piece, width), BF16),
            vmem((nc, piece, width), F32),
            dma,
            dma((2, nr, 3)), dma((2, nr)),
            dma((2, nc)), dma((2, nc)),
            dma((2, nc)), dma((2, nc)),
            dma((2, zn)), dma((2, zn)),
            dma((2, zn)), dma((2, 2, zn)),
            dma((nc,)), dma((nc,)),
            dma((nr,)), dma((nr,)),
            dma((nc,)), dma((nc,)),
        ],
        compiler_params=pltpu.CompilerParams(
            collective_id=0, has_side_effects=True, vmem_limit_bytes=56 * 2**20),
    )(slot_map, features[0], out_grad[0], weight1, weight2, local_tiles)
    return output[None], grad_features[None], gw1, gw2


def solution(mesh):
    placed = (
        P("col", "row", None),
        P(),
        P(),
        P("row", "col", None, None, None),
        P("row", "col", None, None),
        P("row", "col"),
        P("col", "row", None),
    )
    return jax.shard_map(
        functools.partial(on_device, mesh.shape["row"], mesh.shape["col"]),
        mesh=mesh,
        in_specs=placed,
        out_specs=(P("col", "row", None), P("col", "row", None), P(), P()),
        check_vma=False,
    )
```

```python
import functools
import math

import jax
import jax.numpy as jnp
from jax import lax
from jax.experimental import pallas as pl
from jax.experimental.pallas import tpu as pltpu
from jax.sharding import PartitionSpec as P

MESH = pl.DeviceIdType.MESH
BF16 = jnp.bfloat16
F32 = jnp.float32


def dot(a, b, dims=((1,), (0,))):
    return lax.dot_general(a, b, (dims, ((), ())), preferred_element_type=F32)


def kernel(
    nr, nc, factor,
    slot_ref, feat_ref, grad_ref, w1_ref, w2_ref, tiles_hbm,
    out_ref, gf_ref, gw1_ref, gw2_ref,
    tiles, flipped, dense, dense_t, xs, part, psend, precv, pre, hid, agg, zt,
    ybuf, yrecv, zbuf, zrecv, gsend, grecv, gsum, gfin,
    tile_sem, xss, xrs, pss, prs, tss, trs, yss, yrs, zss, zrs,
    g1s, g1r, g2s, g2r, g3s, g3r,
):
    shard, width = feat_ref.shape
    blk = tiles.shape[1]
    panel = dense.shape[1]
    n_tiles = tiles.shape[0] - 1
    zn = nr // 2
    r, c = lax.axis_index("row"), lax.axis_index("col")
    z, y = r // 2, r % 2
    mate = z * 2 + (1 - y)
    piece = 2 * width // nc

    tile_copy = pltpu.make_async_copy(tiles_hbm, tiles.at[pl.ds(0, n_tiles)], tile_sem)
    tile_copy.start()
    xs[0, r] = feat_ref[...]
    xs[1, r] = grad_ref[...]

    barrier = pltpu.get_barrier_semaphore()

    def greet(axis, n, me):
        def body(k, _):
            pl.semaphore_signal(barrier, inc=1, device_id={axis: (me + k) % n}, device_id_type=MESH)
            return 0
        lax.fori_loop(1, n, body, 0)
    greet("row", nr, r)
    greet("col", nc, c)
    pl.semaphore_wait(barrier, nr - 1 + nc - 1)

    def remote(src, dst, ss, rs, axis, target):
        return pltpu.make_async_remote_copy(
            src_ref=src, dst_ref=dst, send_sem=ss, recv_sem=rs,
            device_id={axis: target}, device_id_type=MESH)

    def x_copy(h, idx, way):
        target = (r + 2, r - 2, mate)[way]
        return remote(xs.at[h, idx], xs.at[h, idx], xss.at[h, idx, way], xrs.at[h, idx], "row", target)

    def x_forward(h, idx, sign, act):
        @pl.when(sign > 0)
        def _():
            @pl.when(z < zn - 1)
            def _():
                act(x_copy(h, idx, 0))

        @pl.when(sign < 0)
        def _():
            @pl.when(z > 0)
            def _():
                act(x_copy(h, idx, 1))

    def start(copy):
        copy.start()

    def wait_send(copy):
        copy.wait_send()

    def x_own(h, act):
        act(x_copy(h, r, 2))

        @pl.when(z < zn - 1)
        def _():
            act(x_copy(h, r, 0))

        @pl.when(z > 0)
        def _():
            act(x_copy(h, r, 1))

    rows_step = 512

    def accumulate(h, idx, first=False):
        def body(m, _):
            rows = pl.ds(pl.multiple_of(m * rows_step, rows_step), rows_step)
            add = dot(dense[idx, rows, :], xs[h, idx])
            part[h, rows, :] = add if first else part[h, rows, :] + add
            return 0
        lax.fori_loop(0, panel // rows_step, body, 0)

    def x_pass(h, s):
        def body(q, _):
            sign = 1 - 2 * q
            zz = z - sign * s

            @pl.when((zz >= 0) & (zz < zn))
            def _():
                idx = zz * 2 + y
                x_copy(h, idx, 2).wait_recv()
                x_forward(h, idx, sign, start)
                x_copy(h, idx, 2).start()
            return 0
        lax.fori_loop(0, 2, body, 0)

    def x_use(h, s):
        def body(q, _):
            late = q // 2
            sign = 2 * (q % 2) - 1
            zz = z + sign * (s - late)
            yy = y + late * (1 - 2 * y)

            @pl.when((zz >= 0) & (zz < zn) & ((q < 3) | (s > 1)))
            def _():
                idx = zz * 2 + yy

                @pl.when(late == 1)
                def _():
                    x_copy(h, idx, 2).wait_recv()
                accumulate(h, idx)
            return 0
        lax.fori_loop(0, 4, body, 0)

    def x_steps(h, lo, hi):
        def body(s, _):
            x_pass(h, s)
            x_use(h, s)
            return 0
        lax.fori_loop(lo, hi, body, 0)

    def x_drain(h):
        x_own(h, wait_send)

        def body(k, _):
            q, s = k % 2, k // 2 + 1
            sign = 1 - 2 * q
            zz = z - sign * s

            @pl.when((zz >= 0) & (zz < zn))
            def _():
                idx = zz * 2 + y
                x_forward(h, idx, sign, wait_send)
                x_copy(h, idx, 2).wait_send()
            return 0
        lax.fori_loop(0, 2 * (zn - 1), body, 0)

    def peers(n, me, act):
        def body(k, _):
            act((me + k) % n)
            return 0
        lax.fori_loop(1, n, body, 0)

    def p_copy(h, peer, src):
        return remote(psend.at[h, peer], precv.at[h, src], pss.at[h, peer], prs.at[h, src], "col", peer)

    def own_rows():
        return pl.ds(pl.multiple_of(c * shard, shard), shard)

    def p_send(h):
        def act(peer):
            rows = pl.ds(pl.multiple_of(peer * shard, shard), shard)
            psend[h, peer] = part[h, rows, :].astype(BF16)
            p_copy(h, peer, c).start()
        peers(nc, c, act)

    def p_sum(h):
        agg[h] = part[h, own_rows(), :].astype(BF16).astype(F32)

        def act(peer):
            p_copy(h, peer, peer).wait_recv()
            agg[h] = agg[h] + precv[h, peer].astype(F32)
        peers(nc, c, act)
        return agg[h]

    def t_copy(h, peer, src):
        return remote(zt.at[h, src], zt.at[h, src], tss.at[h, peer], trs.at[h, src], "col", peer)

    def z_send(h, value):
        zt[h, c] = value.astype(BF16)
        peers(nc, c, lambda peer: t_copy(h, peer, c).start())

    def z_wait(h):
        peers(nc, c, lambda peer: t_copy(h, peer, peer).wait_recv())

    def product(h, idx):
        return dot(dense_t[idx], zt[h].reshape(panel, width))

    def y_copy(h, zd):
        return remote(ybuf.at[h, zd], yrecv.at[h, zd], yss.at[h, zd], yrs.at[h, zd], "row", mate)

    def z_copy(h, zd, side):
        target = (r + 2, r - 2)[side]
        return remote(zbuf.at[h, zd], zrecv.at[h, side, zd], zss.at[h, zd], zrs.at[h, side, zd], "row", target)

    def both(d, act):
        def body(q, _):
            zd = z + (2 * q - 1) * d

            @pl.when((zd >= 0) & (zd < zn) & ((q == 0) | (d > 0)))
            def _():
                act(zd)
            return 0
        lax.fori_loop(0, 2, body, 0)

    def y_part(h, d):
        def act(zd):
            ybuf[h, zd] = product(h, zd * 2 + (1 - y)).astype(BF16)
            y_copy(h, zd).start()
        both(d, act)

    def z_part(h, d, total):
        def act(zd):
            total[...] = product(h, zd * 2 + y)
            y_copy(h, zd).wait_recv()
            total[...] = total[...] + yrecv[h, zd].astype(F32)

            @pl.when((z > 0) & (zd >= z))
            def _():
                z_copy(h, zd, 0).wait_recv()
                total[...] = total[...] + zrecv[h, 0, zd].astype(F32)

            @pl.when((z < zn - 1) & (zd <= z))
            def _():
                z_copy(h, zd, 1).wait_recv()
                total[...] = total[...] + zrecv[h, 1, zd].astype(F32)

            @pl.when(zd != z)
            def _():
                zbuf[h, zd] = total[...].astype(BF16)

            @pl.when(zd > z)
            def _():
                z_copy(h, zd, 0).start()

            @pl.when(zd < z)
            def _():
                z_copy(h, zd, 1).start()
        both(d, act)

    def b_steps(h, lo, hi, total):
        def body(i, _):
            @pl.when(i < zn)
            def _():
                y_part(h, zn - 1 - i)

            @pl.when(i >= 1)
            def _():
                z_part(h, zn - i, total)
            return 0
        lax.fori_loop(lo, hi, body, 0)

    def b_drain(h):
        def body(zd, _):
            y_copy(h, zd).wait_send()

            @pl.when(zd > z)
            def _():
                z_copy(h, zd, 0).wait_send()

            @pl.when(zd < z)
            def _():
                z_copy(h, zd, 1).wait_send()
            return 0
        lax.fori_loop(0, zn, body, 0)

    def g1_copy(peer, src):
        return remote(gsend.at[peer], grecv.at[src], g1s.at[peer], g1r.at[src], "col", peer)

    def g2_copy(peer, src):
        return remote(gsum.at[src], gsum.at[src], g2s.at[peer], g2r.at[src], "row", peer)

    def g3_copy(peer, src):
        return remote(gfin.at[src], gfin.at[src], g3s.at[peer], g3r.at[src], "col", peer)

    x_own(0, start)
    tiles[n_tiles] = jnp.zeros((blk, blk), BF16)
    tile_copy.wait()
    per = shard // blk
    n_rows = panel // blk

    def fill(i, _):
        k, row = i // n_rows, i % n_rows
        rows = pl.ds(pl.multiple_of(row * blk, blk), blk)
        for b in range(per):
            slot = slot_ref[row * (nr * per) + k * per + b]
            dense[k, rows, b * blk:(b + 1) * blk] = tiles[slot]
        return 0
    lax.fori_loop(0, nr * n_rows, fill, 0)

    def build_transposed():
        at = lax.broadcasted_iota(jnp.int32, (blk, blk), 0)
        eye = jnp.where(at == lax.broadcasted_iota(jnp.int32, (blk, blk), 1), 1.0, 0.0).astype(BF16)
        group = 8 if n_tiles % 8 == 0 else 1

        def flip(i, _):
            t = i * group
            wide = dot(eye, tiles[pl.ds(t, group)].reshape(group * blk, blk), ((1,), (1,))).astype(BF16)
            for k in range(group):
                flipped[t + k] = wide[:, k * blk:(k + 1) * blk]
            return 0
        lax.fori_loop(0, n_tiles // group, flip, 0)
        flipped[n_tiles] = jnp.zeros((blk, blk), BF16)

        def fill_t(i, _):
            k, b = i // per, i % per
            rows = pl.ds(pl.multiple_of(b * blk, blk), blk)
            for row in range(n_rows):
                slot = slot_ref[row * (nr * per) + i]
                dense_t[k, rows, row * blk:(row + 1) * blk] = flipped[slot]
            return 0
        lax.fori_loop(0, nr * per, fill_t, 0)

    accumulate(0, r, True)
    x_steps(0, 1, zn)
    x_own(1, start)
    x_use(0, zn)
    p_send(0)
    accumulate(1, r, True)
    x_steps(1, 1, 2)

    agg_one = p_sum(0).astype(BF16)
    pre_one = dot(agg_one, w1_ref[...])
    pre[...] = pre_one
    hidden = (pre_one / (1.0 + jnp.exp(-pre_one))).astype(BF16)
    hid[...] = hidden
    z_send(0, dot(hidden, w2_ref[...]))

    x_pass(1, 2)
    build_transposed()
    x_use(1, 2)
    x_steps(1, 3, zn)
    x_use(1, zn)
    p_send(1)
    z_wait(0)

    def with_total(total):
        b_steps(0, 0, 2, total)

        agg_grad = p_sum(1).astype(BF16)
        pre_one = pre[...]
        s = 1.0 / (1.0 + jnp.exp(-pre_one))
        slope = s * (1.0 + pre_one * (1.0 - s))
        grad_pre = (dot(agg_grad, w2_ref[...], ((1,), (1,))) * slope).astype(BF16)
        z_send(1, dot(grad_pre, w1_ref[...], ((1,), (1,))))
        one = dot(agg[0].T.astype(BF16), grad_pre) * factor
        two = dot(hid[...].astype(F32).T.astype(BF16), agg_grad) * factor
        for k in range(nc):
            lo = k * piece
            half = one if lo < width else two
            gsend[k] = half[lo % width:lo % width + piece].astype(BF16)
        peers(nc, c, lambda peer: g1_copy(peer, c).start())

        b_steps(0, 2, zn + 1, total)
        out_ref[...] = total[...].astype(BF16)

        mine = gsend[c].astype(F32)
        gfin[c] = mine

        def add_piece(peer):
            g1_copy(peer, peer).wait_recv()
            gfin[c] = gfin[c] + grecv[peer].astype(F32)
        peers(nc, c, add_piece)
        gsum[r] = gfin[c].astype(BF16)
        peers(nr, r, lambda peer: g2_copy(peer, r).start())

        z_wait(1)
        b_steps(1, 0, 2, total)

        peers(nr, r, lambda peer: g2_copy(peer, peer).wait_recv())
        gfin[c] = gsum[0].astype(F32)

        def add_row(k, _):
            gfin[c] = gfin[c] + gsum[k].astype(F32)
            return 0
        lax.fori_loop(1, nr, add_row, 0)
        peers(nc, c, lambda peer: g3_copy(peer, c).start())

        b_steps(1, 2, zn + 1, total)
        gf_ref[...] = total[...].astype(BF16)

    pl.run_scoped(with_total, pltpu.VMEM((shard, width), F32))

    peers(nc, c, lambda peer: g3_copy(peer, peer).wait_recv())
    for k in range(nc):
        lo = k * piece
        ref = gw1_ref if lo < width else gw2_ref
        ref[lo % width:lo % width + piece, :] = gfin[k]

    for h in range(2):
        x_drain(h)
        peers(nc, c, lambda peer: p_copy(h, peer, c).wait_send())
        peers(nc, c, lambda peer: t_copy(h, peer, c).wait_send())
        b_drain(h)
    peers(nc, c, lambda peer: g1_copy(peer, c).wait_send())
    peers(nr, r, lambda peer: g2_copy(peer, r).wait_send())
    peers(nc, c, lambda peer: g3_copy(peer, c).wait_send())


def write_out(*refs):
    for src, dst in zip(refs[:4], refs[4:]):
        dst[...] = src[...]


def on_device(nr, nc, features, weight1, weight2, tile_values, tile_coords, tile_count, out_grad):
    local_tiles = tile_values[0, 0]
    n_tiles, blk = local_tiles.shape[:2]
    shard, width = features.shape[1:]
    panel, col_blocks = shard * nc, shard * nr // blk
    row_blocks = panel // blk
    slots = jnp.arange(n_tiles, dtype=jnp.int32)
    place = tile_coords[0, 0, 0] * col_blocks + tile_coords[0, 0, 1]
    live = slots < tile_count[0, 0]
    hit = (place[None, :] == jnp.arange(row_blocks * col_blocks, dtype=jnp.int32)[:, None]) & live[None, :]
    slot_map = n_tiles + jnp.sum(jnp.where(hit, slots[None, :] - n_tiles, 0), axis=1)
    zn = nr // 2
    piece = 2 * width // nc
    factor = 1.0 / math.sqrt(shard * nr * nc)
    vmem, dma = pltpu.VMEM, pltpu.SemaphoreType.DMA
    in_vmem = pl.BlockSpec(memory_space=pltpu.VMEM)
    output, grad_features, gw1, gw2 = pl.pallas_call(
        functools.partial(kernel, nr, nc, factor),
        out_shape=(
            jax.ShapeDtypeStruct((shard, width), BF16),
            jax.ShapeDtypeStruct((shard, width), BF16),
            jax.ShapeDtypeStruct((width, width), F32),
            jax.ShapeDtypeStruct((width, width), F32),
        ),
        in_specs=[pl.BlockSpec(memory_space=pltpu.SMEM)] + [in_vmem] * 4 + [pl.BlockSpec(memory_space=pl.ANY)],
        out_specs=(in_vmem,) * 4,
        scratch_shapes=[
            vmem((n_tiles + 1, blk, blk), BF16),
            vmem((n_tiles + 1, blk, blk), BF16),
            vmem((nr, panel, shard), BF16),
            vmem((nr, shard, panel), BF16),
            vmem((2, nr, shard, width), BF16),
            vmem((2, panel, width), F32),
            vmem((2, nc, shard, width), BF16),
            vmem((2, nc, shard, width), BF16),
            vmem((shard, width), F32),
            vmem((shard, width), BF16),
            vmem((2, shard, width), F32),
            vmem((2, nc, shard, width), BF16),
            vmem((2, zn, shard, width), BF16),
            vmem((2, zn, shard, width), BF16),
            vmem((2, zn, shard, width), BF16),
            vmem((2, 2, zn, shard, width), BF16),
            vmem((nc, piece, width), BF16),
            vmem((nc, piece, width), BF16),
            vmem((nr, piece, width), BF16),
            vmem((nc, piece, width), F32),
            dma,
            dma((2, nr, 3)), dma((2, nr)),
            dma((2, nc)), dma((2, nc)),
            dma((2, nc)), dma((2, nc)),
            dma((2, zn)), dma((2, zn)),
            dma((2, zn)), dma((2, 2, zn)),
            dma((nc,)), dma((nc,)),
            dma((nr,)), dma((nr,)),
            dma((nc,)), dma((nc,)),
        ],
        compiler_params=pltpu.CompilerParams(
            collective_id=0, has_side_effects=True, vmem_limit_bytes=56 * 2**20),
    )(slot_map, features[0], out_grad[0], weight1, weight2, local_tiles)
    results = (output, grad_features, gw1, gw2)
    output, grad_features, gw1, gw2 = pl.pallas_call(
        write_out,
        out_shape=tuple(jax.ShapeDtypeStruct(v.shape, v.dtype) for v in results),
        in_specs=[in_vmem] * 4,
        out_specs=(in_vmem,) * 4,
    )(*results)
    return output[None], grad_features[None], gw1, gw2


def solution(mesh):
    placed = (
        P("col", "row", None),
        P(),
        P(),
        P("row", "col", None, None, None),
        P("row", "col", None, None),
        P("row", "col"),
        P("col", "row", None),
    )
    return jax.shard_map(
        functools.partial(on_device, mesh.shape["row"], mesh.shape["col"]),
        mesh=mesh,
        in_specs=placed,
        out_specs=(P("col", "row", None), P("col", "row", None), P(), P()),
        check_vma=False,
    )
```

```python
import functools
import math

import jax
import jax.numpy as jnp
from jax import lax
from jax.experimental import pallas as pl
from jax.experimental.pallas import tpu as pltpu
from jax.sharding import PartitionSpec as P

MESH = pl.DeviceIdType.MESH
BF16 = jnp.bfloat16
F32 = jnp.float32


def dot(a, b, dims=((1,), (0,))):
    return lax.dot_general(a, b, (dims, ((), ())), preferred_element_type=F32)


def kernel(
    nr, nc, factor,
    slot_ref, feat_ref, grad_ref, w1_ref, w2_ref, tiles_hbm,
    out_ref, gf_ref, gw1_ref, gw2_ref,
    tiles, dense, xs, part, psend, precv, pre, hid, agg, zt,
    ybuf, yrecv, zbuf, zrecv, gsend, grecv, gsum, gfin,
    tile_sem, xss, xms, xrs, pss, prs, tss, trs, yss, yrs, zss, zrs,
    g1s, g1r, g2s, g2r, g3s, g3r,
):
    shard, width = feat_ref.shape
    blk = tiles.shape[1]
    panel = dense.shape[1]
    n_tiles = tiles.shape[0] - 1
    zn = nr // 2
    r, c = lax.axis_index("row"), lax.axis_index("col")
    z, y = r // 2, r % 2
    mate = z * 2 + (1 - y)
    piece = 2 * width // nc

    tile_copy = pltpu.make_async_copy(tiles_hbm, tiles.at[pl.ds(0, n_tiles)], tile_sem)
    tile_copy.start()
    xs[0, r] = feat_ref[...]
    xs[1, r] = grad_ref[...]

    barrier = pltpu.get_barrier_semaphore()

    def greet(axis, n, me):
        def body(k, _):
            pl.semaphore_signal(barrier, inc=1, device_id={axis: (me + k) % n}, device_id_type=MESH)
            return 0
        lax.fori_loop(1, n, body, 0)
    greet("row", nr, r)
    greet("col", nc, c)
    pl.semaphore_wait(barrier, nr - 1 + nc - 1)

    def remote(src, dst, ss, rs, axis, target):
        return pltpu.make_async_remote_copy(
            src_ref=src, dst_ref=dst, send_sem=ss, recv_sem=rs,
            device_id={axis: target}, device_id_type=MESH)

    def peers(n, me, act):
        def body(k, _):
            act((me + k) % n)
            return 0
        lax.fori_loop(1, n, body, 0)

    def to_mate(h, idx):
        return remote(xs.at[h, idx], xs.at[h, idx], xms.at[h, idx], xrs.at[h, idx], "row", mate)

    def to_peer(h, zz):
        return remote(xs.at[h, r], xs.at[h, r], xss.at[h, zz], xrs.at[h, r], "row", zz * 2 + y)

    def x_own(h):
        peers(zn, z, lambda zz: to_peer(h, zz).start())
        to_mate(h, r).start()

    def forward(h, k):
        idx = ((z + k) % zn) * 2 + y
        to_mate(h, idx).wait_recv()
        to_mate(h, idx).start()

    def x_drain(h):
        peers(zn, z, lambda zz: to_peer(h, zz).wait_send())

        def body(zz, _):
            to_mate(h, zz * 2 + y).wait_send()
            return 0
        lax.fori_loop(0, zn, body, 0)

    rows_step = 512

    def accumulate(h, idx, first=False):
        def body(m, _):
            rows = pl.ds(pl.multiple_of(m * rows_step, rows_step), rows_step)
            add = dot(dense[idx, rows, :], xs[h, idx])
            part[h, rows, :] = add if first else part[h, rows, :] + add
            return 0
        lax.fori_loop(0, panel // rows_step, body, 0)

    def use(h, k):
        accumulate(h, ((z + k) % zn) * 2 + y)

    def use_mate(h, k):
        idx = ((z + k) % zn) * 2 + (1 - y)
        to_mate(h, idx).wait_recv()
        accumulate(h, idx)

    def loop(lo, hi, act):
        def body(k, _):
            act(k)
            return 0
        lax.fori_loop(lo, hi, body, 0)

    def p_copy(h, peer, src):
        return remote(psend.at[h, peer], precv.at[h, src], pss.at[h, peer], prs.at[h, src], "col", peer)

    def own_rows():
        return pl.ds(pl.multiple_of(c * shard, shard), shard)

    def p_send(h):
        def act(peer):
            rows = pl.ds(pl.multiple_of(peer * shard, shard), shard)
            psend[h, peer] = part[h, rows, :].astype(BF16)
            p_copy(h, peer, c).start()
        peers(nc, c, act)

    def p_sum(h):
        agg[h] = part[h, own_rows(), :].astype(BF16).astype(F32)

        def act(peer):
            p_copy(h, peer, peer).wait_recv()
            agg[h] = agg[h] + precv[h, peer].astype(F32)
        peers(nc, c, act)
        return agg[h]

    def t_copy(h, peer, src):
        return remote(zt.at[h, src], zt.at[h, src], tss.at[h, peer], trs.at[h, src], "col", peer)

    def z_send(h, value):
        zt[h, c] = value.T.astype(BF16)
        peers(nc, c, lambda peer: t_copy(h, peer, c).start())

    def z_wait(h):
        peers(nc, c, lambda peer: t_copy(h, peer, peer).wait_recv())

    def product(h, idx):
        total = dot(zt[h, 0], dense[idx, 0:shard, :])
        for k in range(1, nc):
            total = total + dot(zt[h, k], dense[idx, k * shard:(k + 1) * shard, :])
        return total

    def y_copy(h, zd):
        return remote(ybuf.at[h, zd], yrecv.at[h, zd], yss.at[h, zd], yrs.at[h, zd], "row", mate)

    def z_copy(h, zd, src):
        return remote(zbuf.at[h, zd], zrecv.at[h, src], zss.at[h, zd], zrs.at[h, src], "row", zd * 2 + y)

    def y_parts(h):
        def act(k):
            zd = (z + k) % zn
            ybuf[h, zd] = product(h, zd * 2 + (1 - y)).astype(BF16)
            y_copy(h, zd).start()
        loop(1, zn + 1, act)

    def z_part(h, zd):
        total = product(h, zd * 2 + y)
        y_copy(h, zd).wait_recv()
        return total + yrecv[h, zd].astype(F32)

    def z_parts(h):
        def act(zd):
            zbuf[h, zd] = z_part(h, zd).astype(BF16)
            z_copy(h, zd, z).start()
        peers(zn, z, act)

    def finish(h, total):
        total[...] = z_part(h, z)

        def act(src):
            z_copy(h, src, src).wait_recv()
            total[...] = total[...] + zrecv[h, src].astype(F32)
        peers(zn, z, act)
        return total[...].T.astype(BF16)

    def b_drain(h):
        loop(0, zn, lambda zd: y_copy(h, zd).wait_send())
        peers(zn, z, lambda zd: z_copy(h, zd, z).wait_send())

    def g1_copy(peer, src):
        return remote(gsend.at[peer], grecv.at[src], g1s.at[peer], g1r.at[src], "col", peer)

    def g2_copy(peer, src):
        return remote(gsum.at[src], gsum.at[src], g2s.at[peer], g2r.at[src], "row", peer)

    def g3_copy(peer, src):
        return remote(gfin.at[src], gfin.at[src], g3s.at[peer], g3r.at[src], "col", peer)

    x_own(0)
    tiles[n_tiles] = jnp.zeros((blk, blk), BF16)
    tile_copy.wait()
    per = shard // blk
    n_rows = panel // blk

    def fill(i, _):
        k, row = i // n_rows, i % n_rows
        rows = pl.ds(pl.multiple_of(row * blk, blk), blk)
        for b in range(per):
            slot = slot_ref[row * (nr * per) + k * per + b]
            dense[k, rows, b * blk:(b + 1) * blk] = tiles[slot]
        return 0
    lax.fori_loop(0, nr * n_rows, fill, 0)

    accumulate(0, r, True)
    forward(0, 1)

    def first(k):
        forward(0, k)
        use(0, k - 1)
    loop(2, zn, first)
    x_own(1)
    use(0, zn - 1)
    loop(0, zn - 1, lambda k: use_mate(0, k))
    forward(1, 1)
    use_mate(0, zn - 1)
    p_send(0)
    accumulate(1, r, True)

    def second(k):
        forward(1, k)
        use(1, k - 1)
    loop(2, zn, second)
    use(1, zn - 1)

    agg_one = p_sum(0).astype(BF16)
    pre_one = dot(agg_one, w1_ref[...])
    pre[...] = pre_one
    hidden = (pre_one / (1.0 + jnp.exp(-pre_one))).astype(BF16)
    hid[...] = hidden
    z_send(0, dot(hidden, w2_ref[...]))

    loop(0, zn, lambda k: use_mate(1, k))
    p_send(1)
    z_wait(0)

    def with_total(total):
        y_parts(0)

        agg_grad = p_sum(1).astype(BF16)
        pre_one = pre[...]
        s = 1.0 / (1.0 + jnp.exp(-pre_one))
        slope = s * (1.0 + pre_one * (1.0 - s))
        grad_pre = (dot(agg_grad, w2_ref[...], ((1,), (1,))) * slope).astype(BF16)
        z_send(1, dot(grad_pre, w1_ref[...], ((1,), (1,))))
        one = dot(agg[0].T.astype(BF16), grad_pre) * factor
        two = dot(hid[...].astype(F32).T.astype(BF16), agg_grad) * factor
        for k in range(nc):
            lo = k * piece
            half = one if lo < width else two
            gsend[k] = half[lo % width:lo % width + piece].astype(BF16)
        peers(nc, c, lambda peer: g1_copy(peer, c).start())

        z_parts(0)

        mine = gsend[c].astype(F32)
        gfin[c] = mine

        def add_piece(peer):
            g1_copy(peer, peer).wait_recv()
            gfin[c] = gfin[c] + grecv[peer].astype(F32)
        peers(nc, c, add_piece)
        gsum[r] = gfin[c].astype(BF16)
        peers(nr, r, lambda peer: g2_copy(peer, r).start())

        z_wait(1)
        y_parts(1)
        out_ref[...] = finish(0, total)
        z_parts(1)

        peers(nr, r, lambda peer: g2_copy(peer, peer).wait_recv())
        gfin[c] = gsum[0].astype(F32)

        def add_row(k, _):
            gfin[c] = gfin[c] + gsum[k].astype(F32)
            return 0
        lax.fori_loop(1, nr, add_row, 0)
        peers(nc, c, lambda peer: g3_copy(peer, c).start())

        gf_ref[...] = finish(1, total)

    pl.run_scoped(with_total, pltpu.VMEM((width, shard), F32))

    peers(nc, c, lambda peer: g3_copy(peer, peer).wait_recv())
    for k in range(nc):
        lo = k * piece
        ref = gw1_ref if lo < width else gw2_ref
        ref[lo % width:lo % width + piece, :] = gfin[k]

    for h in range(2):
        x_drain(h)
        peers(nc, c, lambda peer: p_copy(h, peer, c).wait_send())
        peers(nc, c, lambda peer: t_copy(h, peer, c).wait_send())
        b_drain(h)
    peers(nc, c, lambda peer: g1_copy(peer, c).wait_send())
    peers(nr, r, lambda peer: g2_copy(peer, r).wait_send())
    peers(nc, c, lambda peer: g3_copy(peer, c).wait_send())


def write_out(*refs):
    for src, dst in zip(refs[:4], refs[4:]):
        dst[...] = src[...]


def on_device(nr, nc, features, weight1, weight2, tile_values, tile_coords, tile_count, out_grad):
    local_tiles = tile_values[0, 0]
    n_tiles, blk = local_tiles.shape[:2]
    shard, width = features.shape[1:]
    panel, col_blocks = shard * nc, shard * nr // blk
    row_blocks = panel // blk
    slots = jnp.arange(n_tiles, dtype=jnp.int32)
    place = tile_coords[0, 0, 0] * col_blocks + tile_coords[0, 0, 1]
    live = slots < tile_count[0, 0]
    hit = (place[None, :] == jnp.arange(row_blocks * col_blocks, dtype=jnp.int32)[:, None]) & live[None, :]
    slot_map = n_tiles + jnp.sum(jnp.where(hit, slots[None, :] - n_tiles, 0), axis=1)
    zn = nr // 2
    piece = 2 * width // nc
    factor = 1.0 / math.sqrt(shard * nr * nc)
    vmem, dma = pltpu.VMEM, pltpu.SemaphoreType.DMA
    in_vmem = pl.BlockSpec(memory_space=pltpu.VMEM)
    output, grad_features, gw1, gw2 = pl.pallas_call(
        functools.partial(kernel, nr, nc, factor),
        out_shape=(
            jax.ShapeDtypeStruct((shard, width), BF16),
            jax.ShapeDtypeStruct((shard, width), BF16),
            jax.ShapeDtypeStruct((width, width), F32),
            jax.ShapeDtypeStruct((width, width), F32),
        ),
        in_specs=[pl.BlockSpec(memory_space=pltpu.SMEM)] + [in_vmem] * 4 + [pl.BlockSpec(memory_space=pl.ANY)],
        out_specs=(in_vmem,) * 4,
        scratch_shapes=[
            vmem((n_tiles + 1, blk, blk), BF16),
            vmem((nr, panel, shard), BF16),
            vmem((2, nr, shard, width), BF16),
            vmem((2, panel, width), F32),
            vmem((2, nc, shard, width), BF16),
            vmem((2, nc, shard, width), BF16),
            vmem((shard, width), F32),
            vmem((shard, width), BF16),
            vmem((2, shard, width), F32),
            vmem((2, nc, width, shard), BF16),
            vmem((2, zn, width, shard), BF16),
            vmem((2, zn, width, shard), BF16),
            vmem((2, zn, width, shard), BF16),
            vmem((2, zn, width, shard), BF16),
            vmem((nc, piece, width), BF16),
            vmem((nc, piece, width), BF16),
            vmem((nr, piece, width), BF16),
            vmem((nc, piece, width), F32),
            dma,
            dma((2, zn)), dma((2, nr)), dma((2, nr)),
            dma((2, nc)), dma((2, nc)),
            dma((2, nc)), dma((2, nc)),
            dma((2, zn)), dma((2, zn)),
            dma((2, zn)), dma((2, zn)),
            dma((nc,)), dma((nc,)),
            dma((nr,)), dma((nr,)),
            dma((nc,)), dma((nc,)),
        ],
        compiler_params=pltpu.CompilerParams(
            collective_id=0, has_side_effects=True, vmem_limit_bytes=56 * 2**20),
    )(slot_map, features[0], out_grad[0], weight1, weight2, local_tiles)
    results = (output, grad_features, gw1, gw2)
    output, grad_features, gw1, gw2 = pl.pallas_call(
        write_out,
        out_shape=tuple(jax.ShapeDtypeStruct(v.shape, v.dtype) for v in results),
        in_specs=[in_vmem] * 4,
        out_specs=(in_vmem,) * 4,
    )(*results)
    return output[None], grad_features[None], gw1, gw2


def solution(mesh):
    placed = (
        P("col", "row", None),
        P(),
        P(),
        P("row", "col", None, None, None),
        P("row", "col", None, None),
        P("row", "col"),
        P("col", "row", None),
    )
    return jax.shard_map(
        functools.partial(on_device, mesh.shape["row"], mesh.shape["col"]),
        mesh=mesh,
        in_specs=placed,
        out_specs=(P("col", "row", None), P("col", "row", None), P(), P()),
        check_vma=False,
    )
```

```python
import functools
import math

import jax
import jax.numpy as jnp
from jax import lax
from jax.experimental import pallas as pl
from jax.experimental.pallas import tpu as pltpu
from jax.sharding import PartitionSpec as P

MESH = pl.DeviceIdType.MESH
BF16 = jnp.bfloat16
F32 = jnp.float32


def dot(a, b, dims=((1,), (0,))):
    return lax.dot_general(a, b, (dims, ((), ())), preferred_element_type=F32)


def kernel(
    nr, nc, factor,
    slot_ref, feat_ref, grad_ref, w1_ref, w2_ref, tiles_hbm,
    out_ref, gf_ref, gw1_ref, gw2_ref,
    tiles, dense, xs, part, ptwin, pfrom, psend, precv, pre, hid, agg, zt,
    ybuf, yrecv, zbuf, zrecv, gsend, grecv, gsum, gfin,
    tile_sem, xss, xms, xrs, pts, ptr, pss, prs, tss, tts, trs, yss, yrs, zss, zrs,
    g1s, g1r, g2s, g2r, g3s, g3r,
):
    shard, width = feat_ref.shape
    blk = tiles.shape[1]
    panel = dense.shape[1]
    n_tiles = tiles.shape[0] - 1
    zn = nr // 2
    r, c = lax.axis_index("row"), lax.axis_index("col")
    z, y = r // 2, r % 2
    mate = z * 2 + (1 - y)
    xn = nc // 2
    x, core = c // 2, c % 2
    twin = x * 2 + (1 - core)
    piece = 2 * width // nc

    tile_copy = pltpu.make_async_copy(tiles_hbm, tiles.at[pl.ds(0, n_tiles)], tile_sem)
    tile_copy.start()
    xs[0, r] = feat_ref[...]
    xs[1, r] = grad_ref[...]

    barrier = pltpu.get_barrier_semaphore()

    def greet(axis, n, me):
        def body(k, _):
            pl.semaphore_signal(barrier, inc=1, device_id={axis: (me + k) % n}, device_id_type=MESH)
            return 0
        lax.fori_loop(1, n, body, 0)
    greet("row", nr, r)
    greet("col", nc, c)
    pl.semaphore_wait(barrier, nr - 1 + nc - 1)

    def remote(src, dst, ss, rs, axis, target):
        return pltpu.make_async_remote_copy(
            src_ref=src, dst_ref=dst, send_sem=ss, recv_sem=rs,
            device_id={axis: target}, device_id_type=MESH)

    def peers(n, me, act):
        def body(k, _):
            act((me + k) % n)
            return 0
        lax.fori_loop(1, n, body, 0)

    def to_mate(h, idx):
        return remote(xs.at[h, idx], xs.at[h, idx], xms.at[h, idx], xrs.at[h, idx], "row", mate)

    def to_peer(h, zz):
        return remote(xs.at[h, r], xs.at[h, r], xss.at[h, zz], xrs.at[h, r], "row", zz * 2 + y)

    def x_own(h):
        peers(zn, z, lambda zz: to_peer(h, zz).start())
        to_mate(h, r).start()

    def forward(h, k):
        idx = ((z + k) % zn) * 2 + y
        to_mate(h, idx).wait_recv()
        to_mate(h, idx).start()

    def x_drain(h):
        peers(zn, z, lambda zz: to_peer(h, zz).wait_send())

        def body(zz, _):
            to_mate(h, zz * 2 + y).wait_send()
            return 0
        lax.fori_loop(0, zn, body, 0)

    rows_step = min(1024, panel)

    def accumulate(h, idx, first=False):
        def body(m, _):
            rows = pl.ds(pl.multiple_of(m * rows_step, rows_step), rows_step)
            add = dot(dense[idx, rows, :], xs[h, idx])
            part[h, rows, :] = add if first else part[h, rows, :] + add
            return 0
        lax.fori_loop(0, panel // rows_step, body, 0)

    def use(h, k):
        accumulate(h, ((z + k) % zn) * 2 + y)

    def use_mate(h, k):
        idx = ((z + k) % zn) * 2 + (1 - y)
        to_mate(h, idx).wait_recv()
        accumulate(h, idx)

    def loop(lo, hi, act):
        def body(k, _):
            act(k)
            return 0
        lax.fori_loop(lo, hi, body, 0)

    def p_twin(h):
        return remote(ptwin.at[h], pfrom.at[h], pts.at[h], ptr.at[h], "col", twin)

    def p_copy(h, xx, src):
        return remote(psend.at[h, xx], precv.at[h, src], pss.at[h, xx], prs.at[h, src], "col", xx * 2 + core)

    def block_rows(xx, which):
        return pl.ds(pl.multiple_of((xx * 2 + which) * shard, shard), shard)

    def p_start(h):
        def act(xx):
            ptwin[h, xx] = part[h, block_rows(xx, 1 - core), :].astype(BF16)
        loop(0, xn, act)
        p_twin(h).start()

    def p_send(h):
        p_twin(h).wait_recv()

        def act(xx):
            psend[h, xx] = (part[h, block_rows(xx, core), :] + pfrom[h, xx].astype(F32)).astype(BF16)
            p_copy(h, xx, x).start()
        peers(xn, x, act)

    def p_sum(h):
        agg[h] = part[h, block_rows(x, core), :] + pfrom[h, x].astype(F32)

        def act(xx):
            p_copy(h, xx, xx).wait_recv()
            agg[h] = agg[h] + precv[h, xx].astype(F32)
        peers(xn, x, act)
        return agg[h]

    def p_drain(h):
        p_twin(h).wait_send()
        peers(xn, x, lambda xx: p_copy(h, xx, x).wait_send())

    def t_copy(h, xx, src):
        return remote(zt.at[h, src], zt.at[h, src], tss.at[h, xx], trs.at[h, src], "col", xx * 2 + core)

    def t_twin(h, src):
        return remote(zt.at[h, src], zt.at[h, src], tts.at[h, src], trs.at[h, src], "col", twin)

    def z_send(h, value):
        zt[h, c] = value.T.astype(BF16)
        peers(xn, x, lambda xx: t_copy(h, xx, c).start())
        t_twin(h, c).start()

    def z_forward(h):
        def act(xx):
            src = xx * 2 + core
            t_twin(h, src).wait_recv()
            t_twin(h, src).start()
        peers(xn, x, act)

    def z_wait(h):
        loop(0, xn, lambda xx: t_twin(h, xx * 2 + (1 - core)).wait_recv())

    def z_drain(h):
        peers(xn, x, lambda xx: t_copy(h, xx, c).wait_send())
        loop(0, xn, lambda xx: t_twin(h, xx * 2 + core).wait_send())

    def product(h, idx):
        total = dot(zt[h, 0], dense[idx, 0:shard, :])
        for k in range(1, nc):
            total = total + dot(zt[h, k], dense[idx, k * shard:(k + 1) * shard, :])
        return total

    def y_copy(h, zd):
        return remote(ybuf.at[h, zd], yrecv.at[h, zd], yss.at[h, zd], yrs.at[h, zd], "row", mate)

    def z_copy(h, zd, src):
        return remote(zbuf.at[h, zd], zrecv.at[h, src], zss.at[h, zd], zrs.at[h, src], "row", zd * 2 + y)

    def y_parts(h):
        def act(k):
            zd = (z + k) % zn
            ybuf[h, zd] = product(h, zd * 2 + (1 - y)).astype(BF16)
            y_copy(h, zd).start()
        loop(1, zn + 1, act)

    def z_part(h, zd):
        total = product(h, zd * 2 + y)
        y_copy(h, zd).wait_recv()
        return total + yrecv[h, zd].astype(F32)

    def z_parts(h):
        def act(zd):
            zbuf[h, zd] = z_part(h, zd).astype(BF16)
            z_copy(h, zd, z).start()
        peers(zn, z, act)

    def finish(h, total):
        total[...] = z_part(h, z)

        def act(src):
            z_copy(h, src, src).wait_recv()
            total[...] = total[...] + zrecv[h, src].astype(F32)
        peers(zn, z, act)
        return total[...].T.astype(BF16)

    def b_drain(h):
        loop(0, zn, lambda zd: y_copy(h, zd).wait_send())
        peers(zn, z, lambda zd: z_copy(h, zd, z).wait_send())

    def g1_copy(peer, src):
        return remote(gsend.at[peer], grecv.at[src], g1s.at[peer], g1r.at[src], "col", peer)

    def g2_copy(peer, src):
        return remote(gsum.at[src], gsum.at[src], g2s.at[peer], g2r.at[src], "row", peer)

    def g3_copy(peer, src):
        return remote(gfin.at[src], gfin.at[src], g3s.at[peer], g3r.at[src], "col", peer)

    x_own(0)
    tiles[n_tiles] = jnp.zeros((blk, blk), BF16)
    tile_copy.wait()
    per = shard // blk
    n_rows = panel // blk

    group = 4

    def fill(lo, hi):
        def body(i, _):
            k, row = i // (n_rows // group), i % (n_rows // group) * group
            for g in range(group):
                rows = pl.ds(pl.multiple_of((row + g) * blk, blk), blk)
                for b in range(per):
                    slot = slot_ref[(row + g) * (nr * per) + k * per + b]
                    dense[k, rows, b * blk:(b + 1) * blk] = tiles[slot]
            return 0
        lax.fori_loop(lo * (n_rows // group), hi * (n_rows // group), body, 0)

    def first(k):
        fill(2 * k - 2, 2 * k)
        forward(0, k)
    loop(1, zn, first)
    x_own(1)
    fill(nr - 2, nr)
    accumulate(0, r, True)
    loop(1, zn, lambda k: use(0, k))
    loop(0, zn - 1, lambda k: use_mate(0, k))
    forward(1, 1)
    use_mate(0, zn - 1)
    p_start(0)
    accumulate(1, r, True)
    p_send(0)

    def second(k):
        forward(1, k)
        use(1, k - 1)
    loop(2, zn, second)
    use(1, zn - 1)

    agg_one = p_sum(0).astype(BF16)
    pre_one = dot(agg_one, w1_ref[...])
    pre[...] = pre_one
    hidden = (pre_one / (1.0 + jnp.exp(-pre_one))).astype(BF16)
    hid[...] = hidden
    z_send(0, dot(hidden, w2_ref[...]))

    loop(0, zn - 1, lambda k: use_mate(1, k))
    z_forward(0)
    use_mate(1, zn - 1)
    p_start(1)
    z_wait(0)
    p_send(1)

    def with_total(total):
        y_parts(0)

        agg_grad = p_sum(1).astype(BF16)
        pre_one = pre[...]
        s = 1.0 / (1.0 + jnp.exp(-pre_one))
        slope = s * (1.0 + pre_one * (1.0 - s))
        grad_pre = (dot(agg_grad, w2_ref[...], ((1,), (1,))) * slope).astype(BF16)
        z_send(1, dot(grad_pre, w1_ref[...], ((1,), (1,))))
        one = dot(agg[0].T.astype(BF16), grad_pre) * factor
        two = dot(hid[...].astype(F32).T.astype(BF16), agg_grad) * factor
        for k in range(nc):
            lo = k * piece
            half = one if lo < width else two
            gsend[k] = half[lo % width:lo % width + piece].astype(BF16)
        peers(nc, c, lambda peer: g1_copy(peer, c).start())

        z_parts(0)

        mine = gsend[c].astype(F32)
        gfin[c] = mine

        def add_piece(peer):
            g1_copy(peer, peer).wait_recv()
            gfin[c] = gfin[c] + grecv[peer].astype(F32)
        peers(nc, c, add_piece)
        gsum[r] = gfin[c].astype(BF16)
        peers(nr, r, lambda peer: g2_copy(peer, r).start())

        z_forward(1)
        z_wait(1)
        y_parts(1)
        out_ref[...] = finish(0, total)
        z_parts(1)

        peers(nr, r, lambda peer: g2_copy(peer, peer).wait_recv())
        gfin[c] = gsum[0].astype(F32)

        def add_row(k, _):
            gfin[c] = gfin[c] + gsum[k].astype(F32)
            return 0
        lax.fori_loop(1, nr, add_row, 0)
        peers(nc, c, lambda peer: g3_copy(peer, c).start())

        gf_ref[...] = finish(1, total)

    pl.run_scoped(with_total, pltpu.VMEM((width, shard), F32))

    peers(nc, c, lambda peer: g3_copy(peer, peer).wait_recv())
    for k in range(nc):
        lo = k * piece
        ref = gw1_ref if lo < width else gw2_ref
        ref[lo % width:lo % width + piece, :] = gfin[k]

    for h in range(2):
        x_drain(h)
        p_drain(h)
        z_drain(h)
        b_drain(h)
    peers(nc, c, lambda peer: g1_copy(peer, c).wait_send())
    peers(nr, r, lambda peer: g2_copy(peer, r).wait_send())
    peers(nc, c, lambda peer: g3_copy(peer, c).wait_send())


def write_out(*refs):
    for src, dst in zip(refs[:4], refs[4:]):
        dst[...] = src[...]


def on_device(nr, nc, features, weight1, weight2, tile_values, tile_coords, tile_count, out_grad):
    local_tiles = tile_values[0, 0]
    n_tiles, blk = local_tiles.shape[:2]
    shard, width = features.shape[1:]
    panel, col_blocks = shard * nc, shard * nr // blk
    row_blocks = panel // blk
    slots = jnp.arange(n_tiles, dtype=jnp.int32)
    place = tile_coords[0, 0, 0] * col_blocks + tile_coords[0, 0, 1]
    live = slots < tile_count[0, 0]
    hit = (place[None, :] == jnp.arange(row_blocks * col_blocks, dtype=jnp.int32)[:, None]) & live[None, :]
    slot_map = n_tiles + jnp.sum(jnp.where(hit, slots[None, :] - n_tiles, 0), axis=1)
    zn = nr // 2
    piece = 2 * width // nc
    factor = 1.0 / math.sqrt(shard * nr * nc)
    vmem, dma = pltpu.VMEM, pltpu.SemaphoreType.DMA
    in_vmem = pl.BlockSpec(memory_space=pltpu.VMEM)
    output, grad_features, gw1, gw2 = pl.pallas_call(
        functools.partial(kernel, nr, nc, factor),
        out_shape=(
            jax.ShapeDtypeStruct((shard, width), BF16),
            jax.ShapeDtypeStruct((shard, width), BF16),
            jax.ShapeDtypeStruct((width, width), F32),
            jax.ShapeDtypeStruct((width, width), F32),
        ),
        in_specs=[pl.BlockSpec(memory_space=pltpu.SMEM)] + [in_vmem] * 4 + [pl.BlockSpec(memory_space=pl.ANY)],
        out_specs=(in_vmem,) * 4,
        scratch_shapes=[
            vmem((n_tiles + 1, blk, blk), BF16),
            vmem((nr, panel, shard), BF16),
            vmem((2, nr, shard, width), BF16),
            vmem((2, panel, width), F32),
            vmem((2, nc // 2, shard, width), BF16),
            vmem((2, nc // 2, shard, width), BF16),
            vmem((2, nc // 2, shard, width), BF16),
            vmem((2, nc // 2, shard, width), BF16),
            vmem((shard, width), F32),
            vmem((shard, width), BF16),
            vmem((2, shard, width), F32),
            vmem((2, nc, width, shard), BF16),
            vmem((2, zn, width, shard), BF16),
            vmem((2, zn, width, shard), BF16),
            vmem((2, zn, width, shard), BF16),
            vmem((2, zn, width, shard), BF16),
            vmem((nc, piece, width), BF16),
            vmem((nc, piece, width), BF16),
            vmem((nr, piece, width), BF16),
            vmem((nc, piece, width), F32),
            dma,
            dma((2, zn)), dma((2, nr)), dma((2, nr)),
            dma((2,)), dma((2,)), dma((2, nc // 2)), dma((2, nc // 2)),
            dma((2, nc // 2)), dma((2, nc)), dma((2, nc)),
            dma((2, zn)), dma((2, zn)),
            dma((2, zn)), dma((2, zn)),
            dma((nc,)), dma((nc,)),
            dma((nr,)), dma((nr,)),
            dma((nc,)), dma((nc,)),
        ],
        compiler_params=pltpu.CompilerParams(
            collective_id=0, has_side_effects=True, vmem_limit_bytes=56 * 2**20),
    )(slot_map, features[0], out_grad[0], weight1, weight2, local_tiles)
    results = (output, grad_features, gw1, gw2)
    output, grad_features, gw1, gw2 = pl.pallas_call(
        write_out,
        out_shape=tuple(jax.ShapeDtypeStruct(v.shape, v.dtype) for v in results),
        in_specs=[in_vmem] * 4,
        out_specs=(in_vmem,) * 4,
    )(*results)
    return output[None], grad_features[None], gw1, gw2


def solution(mesh):
    placed = (
        P("col", "row", None),
        P(),
        P(),
        P("row", "col", None, None, None),
        P("row", "col", None, None),
        P("row", "col"),
        P("col", "row", None),
    )
    return jax.shard_map(
        functools.partial(on_device, mesh.shape["row"], mesh.shape["col"]),
        mesh=mesh,
        in_specs=placed,
        out_specs=(P("col", "row", None), P("col", "row", None), P(), P()),
        check_vma=False,
    )
```

```python
import functools
import math

import jax
import jax.numpy as jnp
from jax import lax
from jax.experimental import pallas as pl
from jax.experimental.pallas import tpu as pltpu
from jax.sharding import PartitionSpec as P

MESH = pl.DeviceIdType.MESH
BF16 = jnp.bfloat16
F32 = jnp.float32


def dot(a, b, dims=((1,), (0,))):
    return lax.dot_general(a, b, (dims, ((), ())), preferred_element_type=F32)


def kernel(
    nr, nc, factor,
    fwd_ref, bwd_ref, feat_ref, grad_ref, w1_ref, w2_ref, tiles_hbm,
    out_ref, gf_ref, gw1_ref, gw2_ref,
    tiles, sums, xs_a, xs_b, part, ptwin, pfrom, psend, precv, pre, hid, agg, zt_a, zt_b,
    ybuf, yrecv, zbuf, zrecv, gsend, grecv, gsum, gfin,
    tile_sem, xss, xms, xrs, pts, ptr, pss, prs, tss, tts, trs, yss, yrs, zss, zrs,
    g1s, g1r, g2s, g2r, g3s, g3r,
):
    shard, width = feat_ref.shape
    blk = tiles.shape[1]
    panel = part.shape[1]
    n_tiles = tiles.shape[0]
    per = shard // blk
    xs, zt = (xs_a, xs_b), (zt_a, zt_b)
    zn = nr // 2
    r, c = lax.axis_index("row"), lax.axis_index("col")
    z, y = r // 2, r % 2
    mate = z * 2 + (1 - y)
    xn = nc // 2
    x, core = c // 2, c % 2
    twin = x * 2 + (1 - core)
    piece = 2 * width // nc

    tile_copy = pltpu.make_async_copy(tiles_hbm, tiles, tile_sem)
    tile_copy.start()
    xs[0][pl.ds(r * per, per)] = feat_ref[...].reshape(per, blk, width)
    xs[1][pl.ds(r * per, per)] = grad_ref[...].reshape(per, blk, width)

    barrier = pltpu.get_barrier_semaphore()

    def greet(axis, n, me):
        def body(k, _):
            pl.semaphore_signal(barrier, inc=1, device_id={axis: (me + k) % n}, device_id_type=MESH)
            return 0
        lax.fori_loop(1, n, body, 0)
    greet("row", nr, r)
    greet("col", nc, c)
    pl.semaphore_wait(barrier, nr - 1 + nc - 1)

    def remote(src, dst, ss, rs, axis, target):
        return pltpu.make_async_remote_copy(
            src_ref=src, dst_ref=dst, send_sem=ss, recv_sem=rs,
            device_id={axis: target}, device_id_type=MESH)

    def peers(n, me, act):
        def body(k, _):
            act((me + k) % n)
            return 0
        lax.fori_loop(1, n, body, 0)

    def to_mate(h, idx):
        return remote(xs[h].at[pl.ds(idx * per, per)], xs[h].at[pl.ds(idx * per, per)], xms.at[h, idx], xrs.at[h, idx], "row", mate)

    def to_peer(h, zz):
        return remote(xs[h].at[pl.ds(r * per, per)], xs[h].at[pl.ds(r * per, per)], xss.at[h, zz], xrs.at[h, r], "row", zz * 2 + y)

    def x_own(h):
        peers(zn, z, lambda zz: to_peer(h, zz).start())
        to_mate(h, r).start()

    def forward(h, k):
        idx = ((z + k) % zn) * 2 + y
        to_mate(h, idx).wait_recv()
        to_mate(h, idx).start()

    def x_drain(h):
        peers(zn, z, lambda zz: to_peer(h, zz).wait_send())

        def body(zz, _):
            to_mate(h, zz * 2 + y).wait_send()
            return 0
        lax.fori_loop(0, zn, body, 0)

    group = 8 if n_tiles % 8 == 0 else 1

    def segments(ref, at, multiply):
        def body(i, total):
            for g in range(group):
                t = i * group + g
                keep = ref[2 * n_tiles + t].astype(F32)
                total = total * keep + multiply(tiles[ref[t]], ref[n_tiles + t])
                sums[at, t] = total
            return total
        lax.fori_loop(0, n_tiles // group, body, jnp.zeros((blk, blk), F32))
        sums[at, n_tiles] = jnp.zeros((blk, blk), F32)

    def first_product(h):
        segments(fwd_ref, 0, lambda tile, b: dot(tile, xs[h][b]))

        def body(row, _):
            rows = pl.ds(pl.multiple_of(row * blk, blk), blk)
            part[h, rows, :] = sums[0, fwd_ref[3 * n_tiles + row]]
            return 0
        lax.fori_loop(0, panel // blk, body, 0)

    def second_product(h):
        segments(bwd_ref, 1 + h, lambda tile, b: dot(zt[h][b], tile))

    def wait_mates(h):
        loop(0, zn, lambda k: to_mate(h, ((z + k) % zn) * 2 + (1 - y)).wait_recv())

    def loop(lo, hi, act):
        def body(k, _):
            act(k)
            return 0
        lax.fori_loop(lo, hi, body, 0)

    def p_twin(h):
        return remote(ptwin.at[h], pfrom.at[h], pts.at[h], ptr.at[h], "col", twin)

    def p_copy(h, xx, src):
        return remote(psend.at[h, xx], precv.at[h, src], pss.at[h, xx], prs.at[h, src], "col", xx * 2 + core)

    def block_rows(xx, which):
        return pl.ds(pl.multiple_of((xx * 2 + which) * shard, shard), shard)

    def p_start(h):
        def act(xx):
            ptwin[h, xx] = part[h, block_rows(xx, 1 - core), :].astype(BF16)
        loop(0, xn, act)
        p_twin(h).start()

    def p_send(h):
        p_twin(h).wait_recv()

        def act(xx):
            psend[h, xx] = (part[h, block_rows(xx, core), :] + pfrom[h, xx].astype(F32)).astype(BF16)
            p_copy(h, xx, x).start()
        peers(xn, x, act)

    def p_sum(h):
        agg[h] = part[h, block_rows(x, core), :] + pfrom[h, x].astype(F32)

        def act(xx):
            p_copy(h, xx, xx).wait_recv()
            agg[h] = agg[h] + precv[h, xx].astype(F32)
        peers(xn, x, act)
        return agg[h]

    def p_drain(h):
        p_twin(h).wait_send()
        peers(xn, x, lambda xx: p_copy(h, xx, x).wait_send())

    def t_copy(h, xx, src):
        return remote(zt[h].at[pl.ds(src * per, per)], zt[h].at[pl.ds(src * per, per)], tss.at[h, xx], trs.at[h, src], "col", xx * 2 + core)

    def t_twin(h, src):
        return remote(zt[h].at[pl.ds(src * per, per)], zt[h].at[pl.ds(src * per, per)], tts.at[h, src], trs.at[h, src], "col", twin)

    def z_send(h, value):
        flat = value.T.astype(BF16)
        for b in range(per):
            zt[h][c * per + b] = flat[:, b * blk:(b + 1) * blk]
        peers(xn, x, lambda xx: t_copy(h, xx, c).start())
        t_twin(h, c).start()

    def z_forward(h):
        def act(xx):
            src = xx * 2 + core
            t_twin(h, src).wait_recv()
            t_twin(h, src).start()
        peers(xn, x, act)

    def z_wait(h):
        loop(0, xn, lambda xx: t_twin(h, xx * 2 + (1 - core)).wait_recv())

    def z_drain(h):
        peers(xn, x, lambda xx: t_copy(h, xx, c).wait_send())
        loop(0, xn, lambda xx: t_twin(h, xx * 2 + core).wait_send())

    def product(h, idx):
        blocks = [sums[1 + h, bwd_ref[3 * n_tiles + idx * per + b]] for b in range(per)]
        return jnp.concatenate(blocks, axis=1)

    def y_copy(h, zd):
        return remote(ybuf.at[h, zd], yrecv.at[h, zd], yss.at[h, zd], yrs.at[h, zd], "row", mate)

    def z_copy(h, zd, src):
        return remote(zbuf.at[h, zd], zrecv.at[h, src], zss.at[h, zd], zrs.at[h, src], "row", zd * 2 + y)

    def y_parts(h):
        def act(k):
            zd = (z + k) % zn
            ybuf[h, zd] = product(h, zd * 2 + (1 - y)).astype(BF16)
            y_copy(h, zd).start()
        loop(1, zn + 1, act)

    def z_part(h, zd):
        total = product(h, zd * 2 + y)
        y_copy(h, zd).wait_recv()
        return total + yrecv[h, zd].astype(F32)

    def z_parts(h):
        def act(zd):
            zbuf[h, zd] = z_part(h, zd).astype(BF16)
            z_copy(h, zd, z).start()
        peers(zn, z, act)

    def finish(h, total):
        total[...] = z_part(h, z)

        def act(src):
            z_copy(h, src, src).wait_recv()
            total[...] = total[...] + zrecv[h, src].astype(F32)
        peers(zn, z, act)
        return total[...].T.astype(BF16)

    def b_drain(h):
        loop(0, zn, lambda zd: y_copy(h, zd).wait_send())
        peers(zn, z, lambda zd: z_copy(h, zd, z).wait_send())

    def g1_copy(peer, src):
        return remote(gsend.at[peer], grecv.at[src], g1s.at[peer], g1r.at[src], "col", peer)

    def g2_copy(peer, src):
        return remote(gsum.at[src], gsum.at[src], g2s.at[peer], g2r.at[src], "row", peer)

    def g3_copy(peer, src):
        return remote(gfin.at[src], gfin.at[src], g3s.at[peer], g3r.at[src], "col", peer)

    x_own(0)
    loop(1, zn, lambda k: forward(0, k))
    x_own(1)
    tile_copy.wait()
    wait_mates(0)
    first_product(0)
    p_start(0)
    forward(1, 1)
    p_send(0)
    loop(2, zn, lambda k: forward(1, k))

    agg_one = p_sum(0).astype(BF16)
    pre_one = dot(agg_one, w1_ref[...])
    pre[...] = pre_one
    hidden = (pre_one / (1.0 + jnp.exp(-pre_one))).astype(BF16)
    hid[...] = hidden
    z_send(0, dot(hidden, w2_ref[...]))

    z_forward(0)
    z_wait(0)
    second_product(0)
    wait_mates(1)
    first_product(1)
    p_start(1)
    p_send(1)

    def with_total(total):
        y_parts(0)

        agg_grad = p_sum(1).astype(BF16)
        pre_one = pre[...]
        s = 1.0 / (1.0 + jnp.exp(-pre_one))
        slope = s * (1.0 + pre_one * (1.0 - s))
        grad_pre = (dot(agg_grad, w2_ref[...], ((1,), (1,))) * slope).astype(BF16)
        z_send(1, dot(grad_pre, w1_ref[...], ((1,), (1,))))
        one = dot(agg[0].T.astype(BF16), grad_pre) * factor
        two = dot(hid[...].astype(F32).T.astype(BF16), agg_grad) * factor
        for k in range(nc):
            lo = k * piece
            half = one if lo < width else two
            gsend[k] = half[lo % width:lo % width + piece].astype(BF16)
        peers(nc, c, lambda peer: g1_copy(peer, c).start())

        z_parts(0)

        mine = gsend[c].astype(F32)
        gfin[c] = mine

        def add_piece(peer):
            g1_copy(peer, peer).wait_recv()
            gfin[c] = gfin[c] + grecv[peer].astype(F32)
        peers(nc, c, add_piece)
        gsum[r] = gfin[c].astype(BF16)
        peers(nr, r, lambda peer: g2_copy(peer, r).start())

        z_forward(1)
        z_wait(1)
        second_product(1)
        y_parts(1)
        out_ref[...] = finish(0, total)
        z_parts(1)

        peers(nr, r, lambda peer: g2_copy(peer, peer).wait_recv())
        gfin[c] = gsum[0].astype(F32)

        def add_row(k, _):
            gfin[c] = gfin[c] + gsum[k].astype(F32)
            return 0
        lax.fori_loop(1, nr, add_row, 0)
        peers(nc, c, lambda peer: g3_copy(peer, c).start())

        gf_ref[...] = finish(1, total)

    pl.run_scoped(with_total, pltpu.VMEM((width, shard), F32))

    peers(nc, c, lambda peer: g3_copy(peer, peer).wait_recv())
    for k in range(nc):
        lo = k * piece
        ref = gw1_ref if lo < width else gw2_ref
        ref[lo % width:lo % width + piece, :] = gfin[k]

    for h in range(2):
        x_drain(h)
        p_drain(h)
        z_drain(h)
        b_drain(h)
    peers(nc, c, lambda peer: g1_copy(peer, c).wait_send())
    peers(nr, r, lambda peer: g2_copy(peer, r).wait_send())
    peers(nc, c, lambda peer: g3_copy(peer, c).wait_send())


def write_out(*refs):
    for src, dst in zip(refs[:4], refs[4:]):
        dst[...] = src[...]


def on_device(nr, nc, features, weight1, weight2, tile_values, tile_coords, tile_count, out_grad):
    local_tiles = tile_values[0, 0]
    n_tiles, blk = local_tiles.shape[:2]
    shard, width = features.shape[1:]
    panel, col_blocks = shard * nc, shard * nr // blk
    row_blocks = panel // blk
    slots = jnp.arange(n_tiles, dtype=jnp.int32)
    live = slots < tile_count[0, 0]

    def plan(major, minor, blocks):
        major = jnp.where(live, major, blocks)
        key = major * n_tiles + slots
        rank = jnp.sum((key[None, :] < key[:, None]).astype(jnp.int32), axis=1)
        here = rank[None, :] == slots[:, None]
        pick = lambda v: jnp.sum(jnp.where(here, v[None, :], 0), axis=1)
        order = pick(slots * 4096 + major * 64 + minor)
        where = (order // 64) % 64
        keep = (where == jnp.concatenate([jnp.full((1,), -1, jnp.int32), where[:-1]])).astype(jnp.int32)
        ids = jnp.arange(blocks, dtype=jnp.int32)[:, None]
        upto = jnp.sum((major[None, :] <= ids).astype(jnp.int32), axis=1) - 1
        last = jnp.where(jnp.any(major[None, :] == ids, axis=1), upto, n_tiles)
        return jnp.concatenate([order // 4096, order % 64, keep, last])
    rows, cols = tile_coords[0, 0, 0], tile_coords[0, 0, 1]
    by_row, by_col = plan(rows, cols, row_blocks), plan(cols, rows, col_blocks)
    zn = nr // 2
    piece = 2 * width // nc
    factor = 1.0 / math.sqrt(shard * nr * nc)
    vmem, dma = pltpu.VMEM, pltpu.SemaphoreType.DMA
    in_vmem = pl.BlockSpec(memory_space=pltpu.VMEM)
    output, grad_features, gw1, gw2 = pl.pallas_call(
        functools.partial(kernel, nr, nc, factor),
        out_shape=(
            jax.ShapeDtypeStruct((shard, width), BF16),
            jax.ShapeDtypeStruct((shard, width), BF16),
            jax.ShapeDtypeStruct((width, width), F32),
            jax.ShapeDtypeStruct((width, width), F32),
        ),
        in_specs=[pl.BlockSpec(memory_space=pltpu.SMEM)] * 2 + [in_vmem] * 4 + [pl.BlockSpec(memory_space=pl.ANY)],
        out_specs=(in_vmem,) * 4,
        scratch_shapes=[
            vmem((n_tiles, blk, blk), BF16),
            vmem((3, n_tiles + 1, blk, blk), F32),
            vmem((col_blocks, blk, width), BF16),
            vmem((col_blocks, blk, width), BF16),
            vmem((2, panel, width), F32),
            vmem((2, nc // 2, shard, width), BF16),
            vmem((2, nc // 2, shard, width), BF16),
            vmem((2, nc // 2, shard, width), BF16),
            vmem((2, nc // 2, shard, width), BF16),
            vmem((shard, width), F32),
            vmem((shard, width), BF16),
            vmem((2, shard, width), F32),
            vmem((row_blocks, width, blk), BF16),
            vmem((row_blocks, width, blk), BF16),
            vmem((2, zn, width, shard), BF16),
            vmem((2, zn, width, shard), BF16),
            vmem((2, zn, width, shard), BF16),
            vmem((2, zn, width, shard), BF16),
            vmem((nc, piece, width), BF16),
            vmem((nc, piece, width), BF16),
            vmem((nr, piece, width), BF16),
            vmem((nc, piece, width), F32),
            dma,
            dma((2, zn)), dma((2, nr)), dma((2, nr)),
            dma((2,)), dma((2,)), dma((2, nc // 2)), dma((2, nc // 2)),
            dma((2, nc // 2)), dma((2, nc)), dma((2, nc)),
            dma((2, zn)), dma((2, zn)),
            dma((2, zn)), dma((2, zn)),
            dma((nc,)), dma((nc,)),
            dma((nr,)), dma((nr,)),
            dma((nc,)), dma((nc,)),
        ],
        compiler_params=pltpu.CompilerParams(
            collective_id=0, has_side_effects=True, vmem_limit_bytes=56 * 2**20),
    )(by_row, by_col, features[0], out_grad[0], weight1, weight2, local_tiles)
    results = (output, grad_features, gw1, gw2)
    output, grad_features, gw1, gw2 = pl.pallas_call(
        write_out,
        out_shape=tuple(jax.ShapeDtypeStruct(v.shape, v.dtype) for v in results),
        in_specs=[in_vmem] * 4,
        out_specs=(in_vmem,) * 4,
    )(*results)
    return output[None], grad_features[None], gw1, gw2


def solution(mesh):
    placed = (
        P("col", "row", None),
        P(),
        P(),
        P("row", "col", None, None, None),
        P("row", "col", None, None),
        P("row", "col"),
        P("col", "row", None),
    )
    return jax.shard_map(
        functools.partial(on_device, mesh.shape["row"], mesh.shape["col"]),
        mesh=mesh,
        in_specs=placed,
        out_specs=(P("col", "row", None), P("col", "row", None), P(), P()),
        check_vma=False,
    )
```

```python
import functools
import math

import jax
import jax.numpy as jnp
from jax import lax
from jax.experimental import pallas as pl
from jax.experimental.pallas import tpu as pltpu
from jax.sharding import PartitionSpec as P

MESH = pl.DeviceIdType.MESH
BF16 = jnp.bfloat16
F32 = jnp.float32


def dot(a, b, dims=((1,), (0,))):
    return lax.dot_general(a, b, (dims, ((), ())), preferred_element_type=F32)


def kernel(
    nr, nc, factor,
    slot_ref, feat_ref, grad_ref, w1_ref, w2_ref, tiles_hbm,
    out_ref, gf_ref, gw1_ref, gw2_ref,
    tiles, dense, xs, part, ptwin, pfrom, psend, precv, pre, hid, agg, zt,
    ybuf, yrecv, zbuf, zrecv, gsend, grecv, gsum, gfin,
    tile_sem, xss, xms, xrs, pts, ptr, pss, prs, tss, tts, trs, yss, yrs, zss, zrs,
    g1s, g1r, g2s, g2r, g3s, g3r,
):
    shard, width = feat_ref.shape
    blk = tiles.shape[1]
    panel = dense.shape[1]
    n_tiles = tiles.shape[0] - 1
    zn = nr // 2
    r, c = lax.axis_index("row"), lax.axis_index("col")
    z, y = r // 2, r % 2
    mate = z * 2 + (1 - y)
    xn = nc // 2
    x, core = c // 2, c % 2
    twin = x * 2 + (1 - core)
    piece = 2 * width // nc

    tile_copy = pltpu.make_async_copy(tiles_hbm, tiles.at[pl.ds(0, n_tiles)], tile_sem)
    tile_copy.start()
    xs[0, r] = feat_ref[...]
    xs[1, r] = grad_ref[...]

    barrier = pltpu.get_barrier_semaphore()

    def greet(axis, n, me):
        def body(k, _):
            pl.semaphore_signal(barrier, inc=1, device_id={axis: (me + k) % n}, device_id_type=MESH)
            return 0
        lax.fori_loop(1, n, body, 0)
    greet("row", nr, r)
    greet("col", nc, c)
    pl.semaphore_wait(barrier, nr - 1 + nc - 1)

    def remote(src, dst, ss, rs, axis, target):
        return pltpu.make_async_remote_copy(
            src_ref=src, dst_ref=dst, send_sem=ss, recv_sem=rs,
            device_id={axis: target}, device_id_type=MESH)

    def peers(n, me, act):
        def body(k, _):
            act((me + k) % n)
            return 0
        lax.fori_loop(1, n, body, 0)

    def to_mate(h, idx):
        return remote(xs.at[h, idx], xs.at[h, idx], xms.at[h, idx], xrs.at[h, idx], "row", mate)

    def to_peer(h, zz):
        return remote(xs.at[h, r], xs.at[h, r], xss.at[h, zz], xrs.at[h, r], "row", zz * 2 + y)

    def x_own(h):
        peers(zn, z, lambda zz: to_peer(h, zz).start())

    def forward(h, k):
        idx = ((z + k) % zn) * 2 + y
        to_mate(h, idx).wait_recv()
        to_mate(h, idx).start()

    def x_drain(h):
        peers(zn, z, lambda zz: to_peer(h, zz).wait_send())

        def body(zz, _):
            to_mate(h, zz * 2 + y).wait_send()
            return 0
        lax.fori_loop(0, zn, body, 0)

    rows_step = min(1024, panel)

    def accumulate(h, idx, first=False):
        def body(m, _):
            rows = pl.ds(pl.multiple_of(m * rows_step, rows_step), rows_step)
            add = dot(dense[idx, rows, :], xs[h, idx])
            part[h, rows, :] = add if first else part[h, rows, :] + add
            return 0
        lax.fori_loop(0, panel // rows_step, body, 0)

    def use(h, k):
        accumulate(h, ((z + k) % zn) * 2 + y)

    def use_mate(h, k):
        idx = ((z + k) % zn) * 2 + (1 - y)
        to_mate(h, idx).wait_recv()
        accumulate(h, idx)

    def loop(lo, hi, act):
        def body(k, _):
            act(k)
            return 0
        lax.fori_loop(lo, hi, body, 0)

    def p_twin(h):
        return remote(ptwin.at[h], pfrom.at[h], pts.at[h], ptr.at[h], "col", twin)

    def p_copy(h, xx, src):
        return remote(psend.at[h, xx], precv.at[h, src], pss.at[h, xx], prs.at[h, src], "col", xx * 2 + core)

    def block_rows(xx, which):
        return pl.ds(pl.multiple_of((xx * 2 + which) * shard, shard), shard)

    def p_start(h):
        def act(xx):
            ptwin[h, xx] = part[h, block_rows(xx, 1 - core), :].astype(BF16)
        loop(0, xn, act)
        p_twin(h).start()

    def p_send(h):
        p_twin(h).wait_recv()

        def act(xx):
            psend[h, xx] = (part[h, block_rows(xx, core), :] + pfrom[h, xx].astype(F32)).astype(BF16)
            p_copy(h, xx, x).start()
        peers(xn, x, act)

    def p_sum(h):
        agg[h] = part[h, block_rows(x, core), :] + pfrom[h, x].astype(F32)

        def act(xx):
            p_copy(h, xx, xx).wait_recv()
            agg[h] = agg[h] + precv[h, xx].astype(F32)
        peers(xn, x, act)
        return agg[h]

    def p_drain(h):
        p_twin(h).wait_send()
        peers(xn, x, lambda xx: p_copy(h, xx, x).wait_send())

    def t_copy(h, xx, src):
        return remote(zt.at[h, src], zt.at[h, src], tss.at[h, xx], trs.at[h, src], "col", xx * 2 + core)

    def t_twin(h, src):
        return remote(zt.at[h, src], zt.at[h, src], tts.at[h, src], trs.at[h, src], "col", twin)

    def z_send(h, value):
        zt[h, c] = value.T.astype(BF16)
        peers(xn, x, lambda xx: t_copy(h, xx, c).start())
        t_twin(h, c).start()

    def z_forward(h):
        def act(xx):
            src = xx * 2 + core
            t_twin(h, src).wait_recv()
            t_twin(h, src).start()
        peers(xn, x, act)

    def z_wait(h):
        loop(0, xn, lambda xx: t_twin(h, xx * 2 + (1 - core)).wait_recv())

    def z_drain(h):
        peers(xn, x, lambda xx: t_copy(h, xx, c).wait_send())
        loop(0, xn, lambda xx: t_twin(h, xx * 2 + core).wait_send())

    def product(h, idx):
        total = dot(zt[h, 0], dense[idx, 0:shard, :])
        for k in range(1, nc):
            total = total + dot(zt[h, k], dense[idx, k * shard:(k + 1) * shard, :])
        return total

    def y_copy(h, zd):
        return remote(ybuf.at[h, zd], yrecv.at[h, zd], yss.at[h, zd], yrs.at[h, zd], "row", mate)

    def z_copy(h, zd, src):
        return remote(zbuf.at[h, zd], zrecv.at[h, src], zss.at[h, zd], zrs.at[h, src], "row", zd * 2 + y)

    def y_parts(h):
        def act(k):
            zd = (z + k) % zn
            ybuf[h, zd] = product(h, zd * 2 + (1 - y)).astype(BF16)
            y_copy(h, zd).start()
        loop(1, zn + 1, act)

    def z_part(h, zd):
        total = product(h, zd * 2 + y)
        y_copy(h, zd).wait_recv()
        return total + yrecv[h, zd].astype(F32)

    def z_parts(h):
        def act(zd):
            zbuf[h, zd] = z_part(h, zd).astype(BF16)
            z_copy(h, zd, z).start()
        peers(zn, z, act)

    def finish(h, total):
        total[...] = z_part(h, z)

        def act(src):
            z_copy(h, src, src).wait_recv()
            total[...] = total[...] + zrecv[h, src].astype(F32)
        peers(zn, z, act)
        return total[...].T.astype(BF16)

    def b_drain(h):
        loop(0, zn, lambda zd: y_copy(h, zd).wait_send())
        peers(zn, z, lambda zd: z_copy(h, zd, z).wait_send())

    def g1_copy(peer, src):
        return remote(gsend.at[peer], grecv.at[src], g1s.at[peer], g1r.at[src], "col", peer)

    def g2_copy(peer, src):
        return remote(gsum.at[src], gsum.at[src], g2s.at[peer], g2r.at[src], "row", peer)

    def g3_copy(peer, src):
        return remote(gfin.at[src], gfin.at[src], g3s.at[peer], g3r.at[src], "col", peer)

    to_mate(0, r).start()
    x_own(0)
    to_mate(1, r).start()
    tiles[n_tiles] = jnp.zeros((blk, blk), BF16)
    tile_copy.wait()
    per = shard // blk
    n_rows = panel // blk

    group = 4

    def fill(lo, hi):
        def body(i, _):
            k, row = i // (n_rows // group), i % (n_rows // group) * group
            for g in range(group):
                rows = pl.ds(pl.multiple_of((row + g) * blk, blk), blk)
                for b in range(per):
                    slot = slot_ref[(row + g) * (nr * per) + k * per + b]
                    dense[k, rows, b * blk:(b + 1) * blk] = tiles[slot]
            return 0
        lax.fori_loop(lo * (n_rows // group), hi * (n_rows // group), body, 0)

    def first(k):
        fill(2 * k - 2, 2 * k)
        forward(0, k)
    loop(1, zn, first)
    x_own(1)
    fill(nr - 2, nr)
    accumulate(0, r, True)
    loop(1, zn, lambda k: use(0, k))
    loop(0, zn - 1, lambda k: use_mate(0, k))
    forward(1, 1)
    use_mate(0, zn - 1)
    p_start(0)
    accumulate(1, r, True)
    p_send(0)

    def second(k):
        forward(1, k)
        use(1, k - 1)
    loop(2, zn, second)
    use(1, zn - 1)

    agg_one = p_sum(0).astype(BF16)
    pre_one = dot(agg_one, w1_ref[...])
    pre[...] = pre_one
    hidden = (pre_one / (1.0 + jnp.exp(-pre_one))).astype(BF16)
    hid[...] = hidden
    z_send(0, dot(hidden, w2_ref[...]))

    loop(0, zn - 1, lambda k: use_mate(1, k))
    z_forward(0)
    use_mate(1, zn - 1)
    p_start(1)
    z_wait(0)
    p_send(1)

    def with_total(total):
        y_parts(0)

        agg_grad = p_sum(1).astype(BF16)
        pre_one = pre[...]
        s = 1.0 / (1.0 + jnp.exp(-pre_one))
        slope = s * (1.0 + pre_one * (1.0 - s))
        grad_pre = (dot(agg_grad, w2_ref[...], ((1,), (1,))) * slope).astype(BF16)
        z_send(1, dot(grad_pre, w1_ref[...], ((1,), (1,))))
        one = dot(agg[0].T.astype(BF16), grad_pre) * factor
        two = dot(hid[...].astype(F32).T.astype(BF16), agg_grad) * factor
        for k in range(nc):
            lo = k * piece
            half = one if lo < width else two
            gsend[k] = half[lo % width:lo % width + piece].astype(BF16)
        peers(nc, c, lambda peer: g1_copy(peer, c).start())

        z_parts(0)

        mine = gsend[c].astype(F32)
        gfin[c] = mine

        def add_piece(peer):
            g1_copy(peer, peer).wait_recv()
            gfin[c] = gfin[c] + grecv[peer].astype(F32)
        peers(nc, c, add_piece)
        gsum[r] = gfin[c].astype(BF16)
        peers(nr, r, lambda peer: g2_copy(peer, r).start())

        z_forward(1)
        z_wait(1)
        y_parts(1)
        out_ref[...] = finish(0, total)
        z_parts(1)

        peers(nr, r, lambda peer: g2_copy(peer, peer).wait_recv())
        gfin[c] = gsum[0].astype(F32)

        def add_row(k, _):
            gfin[c] = gfin[c] + gsum[k].astype(F32)
            return 0
        lax.fori_loop(1, nr, add_row, 0)
        peers(nc, c, lambda peer: g3_copy(peer, c).start())

        gf_ref[...] = finish(1, total)

    pl.run_scoped(with_total, pltpu.VMEM((width, shard), F32))

    peers(nc, c, lambda peer: g3_copy(peer, peer).wait_recv())
    for k in range(nc):
        lo = k * piece
        ref = gw1_ref if lo < width else gw2_ref
        ref[lo % width:lo % width + piece, :] = gfin[k]

    for h in range(2):
        x_drain(h)
        p_drain(h)
        z_drain(h)
        b_drain(h)
    peers(nc, c, lambda peer: g1_copy(peer, c).wait_send())
    peers(nr, r, lambda peer: g2_copy(peer, r).wait_send())
    peers(nc, c, lambda peer: g3_copy(peer, c).wait_send())


def write_out(*refs):
    for src, dst in zip(refs[:4], refs[4:]):
        dst[...] = src[...]


def on_device(nr, nc, features, weight1, weight2, tile_values, tile_coords, tile_count, out_grad):
    local_tiles = tile_values[0, 0]
    n_tiles, blk = local_tiles.shape[:2]
    shard, width = features.shape[1:]
    panel, col_blocks = shard * nc, shard * nr // blk
    row_blocks = panel // blk
    slots = jnp.arange(n_tiles, dtype=jnp.int32)
    place = tile_coords[0, 0, 0] * col_blocks + tile_coords[0, 0, 1]
    live = slots < tile_count[0, 0]
    hit = (place[None, :] == jnp.arange(row_blocks * col_blocks, dtype=jnp.int32)[:, None]) & live[None, :]
    slot_map = n_tiles + jnp.sum(jnp.where(hit, slots[None, :] - n_tiles, 0), axis=1)
    zn = nr // 2
    piece = 2 * width // nc
    factor = 1.0 / math.sqrt(shard * nr * nc)
    vmem, dma = pltpu.VMEM, pltpu.SemaphoreType.DMA
    in_vmem = pl.BlockSpec(memory_space=pltpu.VMEM)
    output, grad_features, gw1, gw2 = pl.pallas_call(
        functools.partial(kernel, nr, nc, factor),
        out_shape=(
            jax.ShapeDtypeStruct((shard, width), BF16),
            jax.ShapeDtypeStruct((shard, width), BF16),
            jax.ShapeDtypeStruct((width, width), F32),
            jax.ShapeDtypeStruct((width, width), F32),
        ),
        in_specs=[pl.BlockSpec(memory_space=pltpu.SMEM)] + [in_vmem] * 4 + [pl.BlockSpec(memory_space=pl.ANY)],
        out_specs=(in_vmem,) * 4,
        scratch_shapes=[
            vmem((n_tiles + 1, blk, blk), BF16),
            vmem((nr, panel, shard), BF16),
            vmem((2, nr, shard, width), BF16),
            vmem((2, panel, width), F32),
            vmem((2, nc // 2, shard, width), BF16),
            vmem((2, nc // 2, shard, width), BF16),
            vmem((2, nc // 2, shard, width), BF16),
            vmem((2, nc // 2, shard, width), BF16),
            vmem((shard, width), F32),
            vmem((shard, width), BF16),
            vmem((2, shard, width), F32),
            vmem((2, nc, width, shard), BF16),
            vmem((2, zn, width, shard), BF16),
            vmem((2, zn, width, shard), BF16),
            vmem((2, zn, width, shard), BF16),
            vmem((2, zn, width, shard), BF16),
            vmem((nc, piece, width), BF16),
            vmem((nc, piece, width), BF16),
            vmem((nr, piece, width), BF16),
            vmem((nc, piece, width), F32),
            dma,
            dma((2, zn)), dma((2, nr)), dma((2, nr)),
            dma((2,)), dma((2,)), dma((2, nc // 2)), dma((2, nc // 2)),
            dma((2, nc // 2)), dma((2, nc)), dma((2, nc)),
            dma((2, zn)), dma((2, zn)),
            dma((2, zn)), dma((2, zn)),
            dma((nc,)), dma((nc,)),
            dma((nr,)), dma((nr,)),
            dma((nc,)), dma((nc,)),
        ],
        compiler_params=pltpu.CompilerParams(
            collective_id=0, has_side_effects=True, vmem_limit_bytes=56 * 2**20),
    )(slot_map, features[0], out_grad[0], weight1, weight2, local_tiles)
    results = (output, grad_features, gw1, gw2)
    output, grad_features, gw1, gw2 = pl.pallas_call(
        write_out,
        out_shape=tuple(jax.ShapeDtypeStruct(v.shape, v.dtype) for v in results),
        in_specs=[in_vmem] * 4,
        out_specs=(in_vmem,) * 4,
    )(*results)
    return output[None], grad_features[None], gw1, gw2


def solution(mesh):
    placed = (
        P("col", "row", None),
        P(),
        P(),
        P("row", "col", None, None, None),
        P("row", "col", None, None),
        P("row", "col"),
        P("col", "row", None),
    )
    return jax.shard_map(
        functools.partial(on_device, mesh.shape["row"], mesh.shape["col"]),
        mesh=mesh,
        in_specs=placed,
        out_specs=(P("col", "row", None), P("col", "row", None), P(), P()),
        check_vma=False,
    )
```
